128 devices in a mesh: fsdp: 32 (over y, z, core), seq: 4 (over x).
Axes of the slice: x: 4, y: 4, z: 4, core: 2. Of those that a mesh axis runs over, the one named last changes fastest.
Arguments:
- inputs: bfloat16 [32, 512, 512], P('fsdp', 'seq'), may hold values from -6 to 6
- matrices_in: bfloat16 [1, 2, 512, 2048], P(None, None, 'fsdp'), may hold values from -0.25 to 0.25
- matrices_out: bfloat16 [1, 2, 2048, 512], P(None, None, 'fsdp'), may hold values from -0.125 to 0.125
- project_in: bfloat16 [1, 512, 1536], P(None, 'fsdp'), may hold values from -0.25 to 0.25
- project_out: bfloat16 [1, 512, 512], P(None, 'fsdp'), may hold values from -2 to 2
- pos_table: bfloat16 [1, 256, 512], P(None, 'fsdp'), may hold values from -6 to 6
- conv_first: bfloat16 [1, 512, 1024], P(None, 'fsdp'), may hold values from -0.25 to 0.25
- depth_taps: bfloat16 [1, 31, 512], P(None, None, 'fsdp'), may hold values from -1 to 1
- conv_last: bfloat16 [1, 512, 512], P(None, 'fsdp'), may hold values from -0.25 to 0.25
- gain_rows: bfloat16 [1, 6, 512], P(None, None, 'fsdp'), may hold values from 0.5 to 1.5
- shift_rows: bfloat16 [1, 8, 512], P(None, None, 'fsdp'), may hold values from -1.5 to 1.5
- bucket: int32 [1023], replicated, may hold values from 0 to 255
- cotangent: bfloat16 [32, 512, 512], P('fsdp', 'seq'), may hold values from -6 to 6
Outputs:
- output: bfloat16 [32, 512, 512], P('fsdp', 'seq')
- input_grad: float32 [32, 512, 512], P('fsdp', 'seq')
- matrices_in_grad: float32 [1, 2, 512, 2048], P(None, None, 'fsdp')
- matrices_out_grad: float32 [1, 2, 2048, 512], P(None, None, 'fsdp')
- project_in_grad: float32 [1, 512, 1536], P(None, 'fsdp')
- project_out_grad: float32 [1, 512, 512], P(None, 'fsdp')
- pos_table_grad: float32 [1, 256, 512], P(None, 'fsdp')
- conv_first_grad: float32 [1, 512, 1024], P(None, 'fsdp')
- depth_taps_grad: float32 [1, 31, 512], P(None, None, 'fsdp')
- conv_last_grad: float32 [1, 512, 512], P(None, 'fsdp')
- gain_rows_grad: float32 [1, 6, 512], P(None, None, 'fsdp')
- shift_rows_grad: float32 [1, 8, 512], P(None, None, 'fsdp')
The draws below stay inside these ranges and needn't reach their ends.
Inputs may be any that keep to these rules, and one draw needn't show every extreme that they name: Entry o is the bucket of the offset i - j = o - 511.
All inputs are finite; a program needn't handle non-finite values.
Results may differ from the reference program's by a relative error of at most 0.039.
Values may be sent and summed in bfloat16 or wider, within the bound.
No kernel may reach another device: no remote copies, remote signals or barrier semaphores. Data moves between devices by JAX's collectives and lax.ppermute only.
A program may use at most 128 MiB of HBM per device.

```python
import math
import jax
import jax.numpy as jnp
from jax import lax

D = 512
FF = 2048
HEADS = 8
KERNEL = 31
NPOS = 256
LAYERS = 1
SEQS = 32
LEN = 512


def plant(drawn, key, least, high):
    index_at = [jax.random.randint(jax.random.fold_in(key, axis), (), 0, length) for axis, length in enumerate(drawn.shape)]
    longest = drawn.shape.index(max(drawn.shape))
    beside = index_at[:longest] + [(index_at[longest] + 1) % drawn.shape[longest]] + index_at[longest + 1:]
    return drawn.at[tuple(index_at)].set(least).at[tuple(beside)].set(high)


def block_scale(rng, dims, split, low, largest):
    loudness = 1.0
    for position, shards_of in split:
        steps = jax.random.uniform(jax.random.fold_in(jax.random.fold_in(rng, 6), position), (shards_of,), jnp.float32, low / len(split), largest / len(split))
        loudness = loudness * jnp.repeat(jnp.exp(steps), dims[position] // shards_of).reshape((-1,) + (1,) * (len(dims) - 1 - position))
    return loudness


def gaussian(stream_key, extent, width, limit, cuts=(), dtype=jnp.bfloat16):
    array = width * jax.random.normal(stream_key, extent, jnp.float32)
    if cuts:
        array = array * block_scale(stream_key, extent, cuts, -0.22, 0.18)
    return jnp.clip(array, -limit, limit).astype(dtype)


def setup_inputs(seed: int = 0) -> dict:
    seeds = jax.random.split(jax.random.key(seed), 14)
    return {
        "inputs": gaussian(seeds[0], (SEQS, LEN, D), 1.0, 6.0, ((0, 32), (1, 4))),
        "matrices_in": gaussian(seeds[1], (LAYERS, 2, D, FF), D ** -0.5, 0.25, ((2, 32),)),
        "matrices_out": gaussian(seeds[2], (LAYERS, 2, FF, D), FF ** -0.5, 0.125, ((2, 32),)),
        "project_in": gaussian(seeds[3], (LAYERS, D, 3 * D), D ** -0.5, 0.25, ((1, 32),)),
        "project_out": gaussian(seeds[4], (LAYERS, D, D), (D // 64) ** -0.5, 2.0, ((1, 32),)),
        "pos_table": gaussian(seeds[5], (LAYERS, NPOS, D), 1.0, 6.0, ((1, 32),)),
        "conv_first": gaussian(seeds[6], (LAYERS, D, 2 * D), D ** -0.5, 0.25, ((1, 32),)),
        "depth_taps": gaussian(seeds[7], (LAYERS, KERNEL, D), KERNEL ** -0.5, 1.0, ((2, 32),)),
        "conv_last": gaussian(seeds[8], (LAYERS, D, D), D ** -0.5, 0.25, ((1, 32),)),
        "gain_rows": jnp.clip(1.0 + 0.1 * jax.random.normal(seeds[9], (LAYERS, 6, D), jnp.float32), 0.5, 1.5).astype(jnp.bfloat16),
        "shift_rows": gaussian(seeds[10], (LAYERS, 8, D), 0.3, 1.5, ((2, 32),)),
        "bucket": plant(jax.random.randint(seeds[11], (2 * LEN - 1,), 0, NPOS), jax.random.fold_in(seeds[11], 1), 0, NPOS - 1).astype(jnp.int32),
        "cotangent": gaussian(seeds[12], (SEQS, LEN, D), 1.0, 6.0, ((0, 32), (1, 4))),
    }


EPSILON = 1e-05
HIGHEST = lax.Precision.HIGHEST

@jax.custom_vjp
def low(v):
    return lax.optimization_barrier(v.astype(jnp.bfloat16)).astype(jnp.float32)

@jax.custom_vjp
def low_back(v):
    return v

def low_keep(v):
    return (low(v), None)

def low_pass(kept, grad):
    return (grad,)

def back_keep(v):
    return (v, None)

def back_low(kept, grad):
    return (low(grad),)
low.defvjp(low_keep, low_pass)
low_back.defvjp(back_keep, back_low)

def place_offsets(offset_scores, first_row, length):
    heads, rows, wide = offset_scores.shape
    flipped = offset_scores[:, :, ::-1].reshape(heads, rows * wide)
    flipped = jnp.pad(flipped, ((0, 0), (0, length)))
    window = lax.dynamic_slice_in_dim(flipped, length - 1 - first_row, rows * (wide - 1), axis=1)
    return window.reshape(heads, rows, wide - 1)[:, :, :length]

def norm_rows(values, weight_gain, weight_shift):
    centred = values - lax.optimization_barrier(jnp.mean(values, axis=-1, keepdims=True))
    variance = lax.optimization_barrier(jnp.mean(centred * centred, axis=-1, keepdims=True))
    return centred * lax.rsqrt(variance + EPSILON) * weight_gain + weight_shift

def linear(values, matrix):
    return low_back(jnp.einsum('std,df->stf', low(values), matrix, precision=HIGHEST))

def feed_forward(values, weight_gain, weight_shift, matrix_in, matrix_out):
    hidden = linear(norm_rows(values, weight_gain, weight_shift), matrix_in)
    return linear(jax.nn.silu(hidden), matrix_out)

def attend_sequence(member, offset_heads):
    query_u, query_v, key_heads, value_heads = member
    scale_factor = 1.0 / math.sqrt(D // HEADS)
    content = jnp.einsum('ihc,jhc->hij', query_u, key_heads, precision=HIGHEST)
    relative = low_back(jnp.einsum('ihc,ohc->hio', query_v, offset_heads, precision=HIGHEST))
    placed = place_offsets(relative, 0, LEN)
    scores = low_back((content + placed) * scale_factor)
    probs = jax.nn.softmax(scores, axis=-1)
    return low_back(jnp.einsum('hij,jhc->ihc', low(probs), value_heads, precision=HIGHEST))

def attention(values, weight_gain, weight_shift, bias_u, bias_v, matrix_in, matrix_out, table_layer, bucket):
    projected = linear(norm_rows(values, weight_gain, weight_shift), matrix_in)
    query = projected[..., :D]
    heads_shape = (SEQS, LEN, HEADS, D // HEADS)
    query_u = low(query + bias_u).reshape(heads_shape)
    query_v = low(query + bias_v).reshape(heads_shape)
    key_heads = low(projected[..., D:2 * D]).reshape(heads_shape)
    value_heads = low(projected[..., 2 * D:]).reshape(heads_shape)
    offset_heads = jnp.take(table_layer, bucket, axis=0).reshape(2 * LEN - 1, HEADS, D // HEADS)
    stepper = jax.checkpoint(attend_sequence)
    mixed = lax.map(lambda member: stepper(member, offset_heads), (query_u, query_v, key_heads, value_heads))
    return linear(mixed.reshape(SEQS, LEN, D), matrix_out)

def convolve(values, weight_gain, weight_shift, batch_gain, batch_shift, matrix_in, depth_layer, matrix_out):
    gates = linear(norm_rows(values, weight_gain, weight_shift), matrix_in)
    gated = low(gates[..., :D] * jax.nn.sigmoid(gates[..., D:]))
    half_width = KERNEL // 2
    padded = jnp.pad(gated, ((0, 0), (half_width, half_width), (0, 0)))
    mixed = jnp.zeros(gated.shape, jnp.float32)
    for kernel_tap in range(KERNEL):
        mixed = mixed + padded[:, kernel_tap:kernel_tap + LEN] * depth_layer[kernel_tap]
    mixed = low_back(mixed)
    average = lax.optimization_barrier(jnp.mean(mixed, axis=(0, 1)))
    variance = lax.optimization_barrier(jnp.mean(mixed * mixed, axis=(0, 1))) - average * average
    normed = (mixed - average) * lax.rsqrt(variance + EPSILON) * batch_gain + batch_shift
    return linear(jax.nn.silu(normed), matrix_out)

def layer_forward(values, weights, bucket):
    pair_in, pair_out, project_first, project_last, table_layer, conv_start, depth_layer, conv_end, gain_layer, shifts = weights
    values = values + 0.5 * jax.checkpoint(feed_forward)(values, gain_layer[0], shifts[0], pair_in[0], pair_out[0])
    values = values + jax.checkpoint(attention)(values, gain_layer[1], shifts[1], shifts[6], shifts[7], project_first, project_last, table_layer, bucket)
    values = values + jax.checkpoint(convolve)(values, gain_layer[2], shifts[2], gain_layer[5], shifts[5], conv_start, depth_layer, conv_end)
    values = values + 0.5 * jax.checkpoint(feed_forward)(values, gain_layer[3], shifts[3], pair_in[1], pair_out[1])
    return norm_rows(values, gain_layer[4], shifts[4])

def reference(inputs, matrices_in, matrices_out, project_in, project_out, pos_table, conv_first, depth_taps, conv_last, gain_rows, shift_rows, bucket, cotangent):
    weights = (matrices_in.astype(jnp.float32), matrices_out.astype(jnp.float32), project_in.astype(jnp.float32), project_out.astype(jnp.float32), pos_table.astype(jnp.float32), conv_first.astype(jnp.float32), depth_taps.astype(jnp.float32), conv_last.astype(jnp.float32), gain_rows.astype(jnp.float32), shift_rows.astype(jnp.float32))

    def forward(values, weight_list):
        for layer_number in range(LAYERS):
            values = layer_forward(values, [member[layer_number] for member in weight_list], bucket)
        return values
    result, pullback = jax.vjp(forward, inputs.astype(jnp.float32), weights)
    grad_inputs, grad_weights = pullback(cotangent.astype(jnp.float32))
    return (result.astype(jnp.bfloat16), grad_inputs, grad_weights[0], grad_weights[1], grad_weights[2], grad_weights[3], grad_weights[4], grad_weights[5], grad_weights[6], grad_weights[7], grad_weights[8], grad_weights[9])
```

```python
import functools

import jax
import jax.numpy as jnp
from jax import lax
from jax.experimental import pallas as pl
from jax.experimental.pallas import tpu as pltpu
from jax.sharding import Mesh
from jax.sharding import PartitionSpec as P

EPSILON = 1e-05
KERNEL = 31
LEN = 512
WIDTH = 512
CHUNKS = 4
TILE = 128
SPAN = TILE + LEN
FRAMES = 16384
BF = jnp.bfloat16
F32 = jnp.float32
GAIN, SHIFT, TAP = 0, 6, 14
FRONT = 16
PADDED = 560


def dot(left, right):
    return lax.dot_general(left, right, (((1,), (0,)), ((), ())), preferred_element_type=F32)


def dot_right(left, right):
    return lax.dot_general(left, right, (((1,), (1,)), ((), ())), preferred_element_type=F32)


def dot_left(left, right):
    return lax.dot_general(left, right, (((0,), (0,)), ((), ())), preferred_element_type=F32)


def normalise(values):
    centred = values - jnp.mean(values, axis=-1, keepdims=True)
    inverse_root = lax.rsqrt(jnp.mean(centred * centred, axis=-1, keepdims=True) + EPSILON)
    return centred * inverse_root, inverse_root


def norm_back(upstream, normed, inverse_root, gain):
    scaled = upstream * gain
    inner = (
        scaled
        - jnp.mean(scaled, axis=-1, keepdims=True)
        - normed * jnp.mean(scaled * normed, axis=-1, keepdims=True)
    )
    return inverse_root * inner


def column_sum(values):
    return jnp.sum(values, axis=0, keepdims=True)


def row(vec, index):
    return vec[index : index + 1, :]


def flat(block):
    return block.reshape(block.shape[0] * block.shape[1], block.shape[2])


def pieces(out, first, grad):
    for lane in range(grad.shape[1] // 128):
        part = grad[:, lane * 128 : (lane + 1) * 128]
        high = part.shape[0] // 32
        at = first + lane * high
        out[:, at : at + high, :] = part.reshape(32, high, 128).astype(BF)


def lanes(ref, start, size):
    return ref[:, pl.ds(pl.multiple_of(start, 128), size)]


def spread(out, sums):
    for which in range(2):
        for lane in range(4):
            line = sums[which][:, lane * 128 : (lane + 1) * 128]
            out[:, 4 * which + lane, :] = jnp.broadcast_to(line, (32, 128))


def collect(stats):
    total = jnp.sum(stats[...], axis=0)
    return [
        jnp.concatenate([total[4 * which + lane : 4 * which + lane + 1] for lane in range(4)], axis=1)
        for which in range(2)
    ]


def feed_front(x, vec, matrix_in, matrix_out, project, x1, hidden, query_u, query_v, key, value, fed, total):
    values = x[...].astype(F32)
    normed, _ = normalise(values)
    fed[...] = (normed * row(vec, GAIN) + row(vec, SHIFT)).astype(BF)
    for j in range(CHUNKS):
        part = dot(fed[...], flat(matrix_in[:, 16 * j : 16 * j + 16, :]))
        hidden[j] = part.astype(BF)
        active = (part * jax.nn.sigmoid(part)).astype(BF)
        grown = dot(active, flat(matrix_out[8 * j : 8 * j + 8]))
        total[...] = grown if j == 0 else total[...] + grown
    after = values + 0.5 * total[...]
    x1[...] = after
    normed, _ = normalise(after)
    fed[...] = (normed * row(vec, GAIN + 1) + row(vec, SHIFT + 1)).astype(BF)
    query = dot(fed[...], flat(project[:, 0:16, :]))
    query_u[...] = (query + row(vec, SHIFT + 6)).astype(BF)
    query_v[...] = (query + row(vec, SHIFT + 7)).astype(BF)
    key[...] = dot(fed[...], flat(project[:, 16:32, :])).astype(BF)
    value[...] = dot(fed[...], flat(project[:, 32:48, :])).astype(BF)


def head_mask(which, rows):
    lane = lax.broadcasted_iota(jnp.int32, (rows, 128), 1)
    return (lane < 64) if which == 0 else (lane >= 64)


def attend(query_u, query_v, key, value, table, bucket, probs, mixed, offsets, chosen, scores):
    @pl.when(pl.program_id(0) == 0)
    def _():
        number = lax.broadcasted_iota(jnp.int32, (2 * LEN, 256), 1)
        chosen[...] = (bucket[...] == number).astype(F32).astype(BF)

    offsets[...] = dot(chosen[...], table[...]).astype(BF)
    for head in range(2):
        mask = head_mask(head, LEN)
        content = jnp.where(mask, query_u[...], 0.0).astype(BF)
        place = jnp.where(mask, query_v[...], 0.0).astype(BF)
        scores[...] = dot_right(content, key[...])
        for t in range(4):
            rows = slice(t * TILE, (t + 1) * TILE)
            start = LEN - TILE - TILE * t
            relative = dot_right(place[rows], offsets[start : start + SPAN, :])
            relative = pltpu.roll(relative, SPAN - TILE + 1, 1, stride=1, stride_axis=0)
            logits = (scores[rows, :] + relative[:, :LEN]) * 0.125
            expo = jnp.exp(logits - jnp.max(logits, axis=1, keepdims=True))
            probs_low = (expo / jnp.sum(expo, axis=1, keepdims=True)).astype(BF)
            probs[head, rows, :] = probs_low
            out = dot(probs_low, value[...]).astype(BF)
            if head == 0:
                mixed[rows, :] = out
            else:
                mixed[rows, :] = jnp.where(head_mask(0, TILE), mixed[rows, :], out)


def depthwise(padded, vec, out, flip):
    def step(index, carry):
        lane = pl.multiple_of((index % 4) * 128, 128)
        first = pl.multiple_of((index // 4) * 64, 64)
        window = padded[pl.ds(first, 96), pl.ds(lane, 128)]
        total = None
        for shift in range(8):
            part = None
            for q in range(4):
                tap = 8 * q + shift - 1
                if tap < 0 or tap >= KERNEL:
                    continue
                tap = KERNEL - 1 - tap if flip else tap
                term = window[8 * q : 8 * q + 72] * vec[TAP + tap : TAP + tap + 1, pl.ds(lane, 128)]
                part = term if part is None else part + term
            part = part[shift : shift + 64]
            total = part if total is None else total + part
        out[pl.ds(first, 64), pl.ds(lane, 128)] = total
        return carry

    lax.fori_loop(0, 32, step, 0)


def fill(padded, values):
    padded[0:FRONT, :] = jnp.zeros((FRONT, WIDTH), F32)
    padded[FRONT : FRONT + LEN, :] = values
    padded[FRONT + LEN :, :] = jnp.zeros((PADDED - FRONT - LEN, WIDTH), F32)


def conv_front(mixed, x1, project, first, vec, x2, gates, gated, deep, stats, padded):
    after = x1[...] + dot(mixed[...], flat(project[...]))
    x2[...] = after
    normed, _ = normalise(after)
    conv_in = (normed * row(vec, GAIN + 2) + row(vec, SHIFT + 2)).astype(BF)
    half = dot(conv_in, flat(first[:, 0:16, :]))
    gate = dot(conv_in, flat(first[:, 16:32, :]))
    gates[0] = half.astype(BF)
    gates[1] = gate.astype(BF)
    low = (half * jax.nn.sigmoid(gate)).astype(BF)
    gated[...] = low
    fill(padded, low.astype(F32))
    depthwise(padded, vec, deep, False)
    values = deep[...]
    spread(stats, (column_sum(values), column_sum(values * values)))


def batch_norm(stats, deep, vec):
    total, square = collect(stats)
    average = total / FRAMES
    inverse_root = lax.rsqrt(square / FRAMES - average * average + EPSILON)
    return (deep - average) * inverse_root, inverse_root


def feed_back(upstream, fed, hidden, matrix_in, matrix_out, grads, first, u_low, grown, total, quarter):
    u_low[...] = upstream.astype(BF)
    side = lanes(u_low, quarter * 128, 128)
    for j in range(CHUNKS):
        part = hidden[j].astype(F32)
        logistic = jax.nn.sigmoid(part)
        active = (part * logistic).astype(BF)
        out_grad = dot_left(active, side)
        grads[8 * j : 8 * j + 8, first + 64 : first + 128, :] = out_grad.reshape(8, 64, 128).astype(BF)
        slope = logistic * (1.0 + part * (1.0 - logistic))
        grown[...] = (dot_right(u_low[...], flat(matrix_out[8 * j : 8 * j + 8])) * slope).astype(BF)

        @pl.when(quarter == j)
        def _():
            pieces(grads, first, dot_left(fed[...], grown[...]))

        back = dot_right(grown[...], flat(matrix_in[:, 16 * j : 16 * j + 16, :]))
        total[...] = back if j == 0 else total[...] + back


def centre(
    where, deep, stats, x2, last, matrix_in, matrix_out, vec, cotangent,
    y, gx3, before_grad, stats_back, grads, sums,
    fed, hidden, total, u_low, grown, wide,
):
    quarter = where[0]
    own = pl.ds(pl.multiple_of(quarter * TILE, TILE), TILE)
    centred, _ = batch_norm(stats, deep[...], vec)
    before = centred * row(vec, GAIN + 5) + row(vec, SHIFT + 5)
    swish = (before * jax.nn.sigmoid(before)).astype(BF)
    x3 = x2[...] + dot(swish, flat(last[...]))
    wide[...] = x3
    normed, inverse_root = normalise(x3)
    fed[...] = (normed * row(vec, GAIN + 3) + row(vec, SHIFT + 3)).astype(BF)
    for j in range(CHUNKS):
        part = dot(fed[...], flat(matrix_in[:, 16 * j : 16 * j + 16, :]))
        hidden[j] = part.astype(BF)
        active = (part * jax.nn.sigmoid(part)).astype(BF)
        out = dot(active, flat(matrix_out[8 * j : 8 * j + 8]))
        total[...] = out if j == 0 else total[...] + out
    x4 = wide[...] + 0.5 * total[...]
    normed4, inverse4 = normalise(x4)
    gx3[...] = normed4 * row(vec, GAIN + 4) + row(vec, SHIFT + 4)
    y[...] = gx3[own, :].astype(BF)
    upstream = cotangent[...].astype(F32)
    sums[...] = jnp.zeros_like(sums)
    sums[2:3, :] = column_sum(upstream * normed4)
    sums[3:4, :] = column_sum(upstream)
    gx4 = norm_back(upstream, normed4, inverse4, row(vec, GAIN + 4))
    gx3[...] = gx4
    feed_back(0.5 * gx4, fed, hidden, matrix_in, matrix_out, grads, 0, u_low, grown, total, quarter)
    upstream = total[...]
    normed, inverse_root = normalise(wide[...])
    sums[0:1, :] = column_sum(upstream * normed)
    sums[1:2, :] = column_sum(upstream)
    after = gx3[...] + norm_back(upstream, normed, inverse_root, row(vec, GAIN + 3))
    gx3[...] = after
    u_low[...] = after.astype(BF)
    centred, _ = batch_norm(stats, deep[...], vec)
    before = centred * row(vec, GAIN + 5) + row(vec, SHIFT + 5)
    logistic = jax.nn.sigmoid(before)
    swish = (before * logistic).astype(BF)
    pieces(grads, 128, dot_left(swish, lanes(u_low, quarter * 128, 128)))
    slope = logistic * (1.0 + before * (1.0 - logistic))
    back = dot_right(u_low[...], flat(last[...])) * slope
    before_grad[...] = back
    shift_sum, gain_sum = column_sum(back), column_sum(back * centred)
    sums[4:5, :] = gain_sum
    sums[5:6, :] = shift_sum
    spread(stats_back, (shift_sum, gain_sum))


def tap_grads(padded, padded_grad, acc):
    acc[...] = jnp.zeros_like(acc)

    def step(index, carry):
        lane = pl.multiple_of((index % 4) * 128, 128)
        first = pl.multiple_of((index // 4) * 104, 8)
        grad = padded_grad[pl.ds(first + 8, 112), pl.ds(lane, 128)]
        window = padded[pl.ds(first, 128), pl.ds(lane, 128)]
        for shift in range(8):
            moved = grad[8 - shift : 112 - shift]
            for q in range(4):
                tap = 8 * q + shift - 1
                if tap < 0 or tap >= KERNEL:
                    continue
                term = (window[8 * q : 8 * q + 104] * moved).reshape(13, 8, 128)
                acc[tap, :, pl.ds(lane, 128)] += jnp.sum(term, axis=0)
        return carry

    lax.fori_loop(0, 20, step, 0)


def conv_back(
    where, before_grad, stats_back, stats, deep, gated, gates, x2, gx3, first, project, mixed, vec,
    gx2, mixed_grad, grads, sums,
    padded, padded_grad, total, acc, both, u_low,
):
    quarter = where[0]
    centred, inverse_root = batch_norm(stats, deep[...], vec)
    shift_sum, gain_sum = collect(stats_back)
    inner = before_grad[...] - shift_sum / FRAMES - centred * (gain_sum / FRAMES)
    low = (inverse_root * row(vec, GAIN + 5) * inner).astype(BF)
    fill(padded_grad, low.astype(F32))
    fill(padded, gated[...].astype(F32))
    depthwise(padded_grad, vec, total, True)
    tap_grads(padded, padded_grad, acc)
    sums[...] = jnp.zeros_like(sums)
    for tap in range(KERNEL):
        sums[8 + tap : 9 + tap, :] = column_sum(acc[tap])
    opened = jax.nn.sigmoid(gates[1].astype(F32))
    passed = total[...] * opened
    both[:, 0:WIDTH] = passed.astype(BF)
    both[:, WIDTH:] = (passed * gates[0].astype(F32) * (1.0 - opened)).astype(BF)
    normed, inverse_root = normalise(x2[...])
    conv_in = (normed * row(vec, GAIN + 2) + row(vec, SHIFT + 2)).astype(BF)
    pieces(grads, 0, dot_left(conv_in, lanes(both, quarter * 256, 256)))
    upstream = dot_right(both[:, 0:WIDTH], flat(first[:, 0:16, :]))
    upstream = upstream + dot_right(both[:, WIDTH:], flat(first[:, 16:32, :]))
    sums[0:1, :] = column_sum(upstream * normed)
    sums[1:2, :] = column_sum(upstream)
    after = gx3[...] + norm_back(upstream, normed, inverse_root, row(vec, GAIN + 2))
    gx2[...] = after
    u_low[...] = after.astype(BF)
    pieces(grads, 32, dot_left(mixed[...], lanes(u_low, quarter * 128, 128)))
    mixed_grad[...] = dot_right(u_low[...], flat(project[...])).astype(BF)


def attend_back(
    where, query_u, query_v, key, value, mixed_grad, probs, offsets, bucket,
    query_grad, key_grad, value_grad, sums, grads,
    score_grad, u_grad, v_grad, offset_grad,
):
    mine = where[0] == pl.program_id(0)
    row_at = lax.broadcasted_iota(jnp.int32, (TILE, TILE), 0)
    column_at = lax.broadcasted_iota(jnp.int32, (TILE, TILE), 1)
    mirror = (row_at + column_at == TILE - 1).astype(F32).astype(BF)
    left = head_mask(0, LEN)
    left_tile = head_mask(0, TILE)

    @pl.when(mine)
    def _():
        offset_grad[...] = jnp.zeros_like(offset_grad)

    for head in range(2):
        mask = head_mask(head, LEN)
        upstream = jnp.where(mask, mixed_grad[...], 0.0).astype(BF)
        place = jnp.where(mask, query_v[...], 0.0).astype(BF)
        for t in range(4):
            rows = slice(t * TILE, (t + 1) * TILE)
            start = LEN - TILE - TILE * t
            window = slice(start, start + SPAN)
            prob_grad = dot_right(upstream[rows], value[...])
            chance = probs[head, rows, :].astype(F32)
            weighed = jnp.sum(chance * prob_grad, axis=1, keepdims=True)
            low = (chance * (prob_grad - weighed)).astype(BF)
            score_grad[rows, :] = low
            u_part = dot(low, key[...])
            mirrored = dot(mirror, low) * 0.125
            mirrored = jnp.concatenate([mirrored, jnp.zeros((TILE, TILE), F32)], axis=1)
            placed = pltpu.roll(mirrored, 0, 1, stride=1, stride_axis=0).astype(BF)
            relative = dot(mirror, placed).astype(BF)
            v_part = dot(relative, offsets[window, :])
            if head == 0:
                u_grad[rows, :] = u_part
                v_grad[rows, :] = v_part
            else:
                u_grad[rows, :] = jnp.where(left_tile, u_grad[rows, :], u_part)
                v_grad[rows, :] = jnp.where(left_tile, v_grad[rows, :], v_part)

            @pl.when(mine)
            def _():
                offset_grad[window, :] += dot_left(relative, place[rows])

        key_part = dot_left(score_grad[...], query_u[...]) * 0.125
        value_part = dot_left(probs[head], upstream)
        if head == 0:
            key_grad[...] = key_part.astype(BF)
            value_grad[...] = value_part.astype(BF)
        else:
            key_grad[...] = jnp.where(left, key_grad[...], key_part.astype(BF))
            value_grad[...] = jnp.where(left, value_grad[...], value_part.astype(BF))
    from_u, from_v = u_grad[...] * 0.125, v_grad[...]
    query_grad[...] = (from_u + from_v).astype(BF)
    sums[...] = jnp.zeros_like(sums)
    sums[0:1, :] = column_sum(from_u)
    sums[1:2, :] = column_sum(from_v)

    @pl.when(mine)
    def _():
        number = lax.broadcasted_iota(jnp.int32, (256, 2 * LEN), 0)
        chosen = (bucket[...] == number).astype(F32).astype(BF)
        table_grad = dot(chosen, offset_grad[...].astype(BF)).reshape(32, 8, 128)
        grads[...] = jnp.concatenate([table_grad, jnp.zeros((32, 8, 128), F32)], axis=1).astype(BF)


def feed_last(
    where, query_grad, key_grad, value_grad, x1, gx2, project, matrix_in, matrix_out, hidden, x, vec,
    sums4, sums5, sums6,
    gx0, grads,
    three, fed, total, u_low, grown, wide, packed,
):
    quarter = where[0]
    own = pl.ds(pl.multiple_of(quarter * TILE, TILE), TILE)
    three[:, 0:WIDTH] = query_grad[...]
    three[:, WIDTH : 2 * WIDTH] = key_grad[...]
    three[:, 2 * WIDTH :] = value_grad[...]
    packed[...] = jnp.zeros_like(packed)
    normed, inverse_root = normalise(x1[...])
    attn_in = (normed * row(vec, GAIN + 1) + row(vec, SHIFT + 1)).astype(BF)
    pieces(grads, 128, dot_left(attn_in, lanes(three, quarter * 384, 384)))
    upstream = dot_right(query_grad[...], flat(project[:, 0:16, :]))
    upstream = upstream + dot_right(key_grad[...], flat(project[:, 16:32, :]))
    upstream = upstream + dot_right(value_grad[...], flat(project[:, 32:48, :]))
    packed[GAIN + 1 : GAIN + 2, :] = column_sum(upstream * normed)
    packed[SHIFT + 1 : SHIFT + 2, :] = column_sum(upstream)
    gx1 = gx2[...] + norm_back(upstream, normed, inverse_root, row(vec, GAIN + 1))
    wide[...] = gx1
    normed, inverse_root = normalise(x[...].astype(F32))
    fed[...] = (normed * row(vec, GAIN) + row(vec, SHIFT)).astype(BF)
    feed_back(0.5 * gx1, fed, hidden, matrix_in, matrix_out, grads, 0, u_low, grown, total, quarter)
    upstream = total[...]
    normed, inverse_root = normalise(x[...].astype(F32))
    packed[GAIN : GAIN + 1, :] = column_sum(upstream * normed)
    packed[SHIFT : SHIFT + 1, :] = column_sum(upstream)
    wide[...] = wide[...] + norm_back(upstream, normed, inverse_root, row(vec, GAIN))
    gx0[...] = wide[own, :]
    packed[GAIN + 2 : GAIN + 3, :] = row(sums5, 0)
    packed[SHIFT + 2 : SHIFT + 3, :] = row(sums5, 1)
    packed[TAP : TAP + KERNEL, :] = sums5[8 : 8 + KERNEL, :]
    for index in range(3):
        packed[GAIN + 3 + index : GAIN + 4 + index, :] = row(sums4, 2 * index)
        packed[SHIFT + 3 + index : SHIFT + 4 + index, :] = row(sums4, 2 * index + 1)
    packed[SHIFT + 6 : SHIFT + 8, :] = sums6[0:2, :]
    pieces(grads, 176, packed[...].T)


def unpack(parts, g_in, g_out, g_project, g_last, g_table, g_first, g_taps, g_conv, g_gain, g_shift):
    def take(first, rows, side):
        return parts[side, first : first + rows, :].astype(F32)

    for side in range(4):
        for m, base in ((0, 208), (1, 0)):
            for lane in range(4):
                column = side * 512 + lane * 128
                g_in[m, :, column : column + 128] = take(base + 16 * lane, 16, side)
            g_out[m, :, side * 128 : side * 128 + 128] = take(base + 64, 64, side)
        for lane in range(3):
            column = side * 384 + lane * 128
            g_project[:, column : column + 128] = take(336 + 16 * lane, 16, side)
        for lane in range(2):
            column = side * 256 + lane * 128
            g_first[:, column : column + 128] = take(144 + 16 * lane, 16, side)
        lane = slice(side * 128, side * 128 + 128)
        g_last[:, lane] = take(176, 16, side)
        g_conv[:, lane] = take(128, 16, side)
        g_table[:, lane] = take(192, 16, side)[0:8]
    vectors = take(384, 16, 0).T
    g_gain[...] = vectors[GAIN : GAIN + 6]
    g_shift[...] = vectors[SHIFT : SHIFT + 8]
    g_taps[...] = vectors[TAP : TAP + KERNEL]


def whole(shape):
    return pl.BlockSpec(shape, lambda *at: (0,) * len(shape))


def rows_of(first, size):
    return pl.BlockSpec((32, size, WIDTH), lambda *at: (0, first // size, 0))


def pair():
    return pl.BlockSpec((LEN, 128), lambda h: (0, h))


WHERE = pl.BlockSpec(memory_space=pltpu.SMEM)
FULL = (LEN, WIDTH)


def call(kernel, in_specs, outs, scratch, grid=(1,), out_specs=None):
    return pl.pallas_call(
        kernel,
        grid=grid,
        in_specs=in_specs,
        out_specs=out_specs or [whole(shape) for shape, _ in outs],
        out_shape=[jax.ShapeDtypeStruct(shape, dtype) for shape, dtype in outs],
        scratch_shapes=[pltpu.VMEM(shape, dtype) for shape, dtype in scratch],
        compiler_params=pltpu.CompilerParams(vmem_limit_bytes=56 << 20),
    )


def share(stats):
    return lax.all_to_all(stats, ("y", "z", "c"), 0, 0, tiled=True)


def shards(
    inputs, matrices_in, matrices_out, project_in, project_out, pos_table, conv_first, depth_taps,
    conv_last, gain_rows, shift_rows, bucket, cotangent,
):
    fsdp = ("y", "z", "c")
    where = lax.axis_index("x").reshape(1).astype(jnp.int32)

    def columns(matrix, count):
        return [matrix[:, 512 * j : 512 * j + 512] for j in range(count)]

    packed = jnp.concatenate(
        columns(matrices_in[0, 0], 4)
        + columns(matrices_in[0, 1], 4)
        + [matrices_out[0, 0], matrices_out[0, 1]]
        + columns(project_in[0], 3)
        + [project_out[0]]
        + columns(conv_first[0], 2)
        + [conv_last[0], pos_table[0], jnp.zeros((8, 512), BF)],
        axis=0,
    )
    weights = lax.all_gather(packed, fsdp, axis=0, tiled=False)
    small = jnp.concatenate(
        [gain_rows[0], shift_rows[0], depth_taps[0], jnp.zeros((3, 16), BF)], axis=0
    )
    vec = lax.all_gather(small, fsdp, axis=1, tiled=True).astype(F32)
    frames = lax.all_gather(
        jnp.concatenate([inputs[0], cotangent[0]], axis=1), "x", axis=0, tiled=True
    )
    table = weights[:, 368:376, :].reshape(256, WIDTH)
    reversed_bucket = jnp.concatenate([bucket[::-1], jnp.full((1,), -1, jnp.int32)])
    tall, long = reversed_bucket.reshape(2 * LEN, 1), reversed_bucket.reshape(1, 2 * LEN)

    vec_spec = whole((48, WIDTH))
    full = whole(FULL)
    stats_spec = whole((32, 8, 128))
    x_spec = pl.BlockSpec(FULL, lambda *at: (0, 0))
    cotangent_spec = pl.BlockSpec(FULL, lambda *at: (0, 1))
    in_specs = [rows_of(64 * m, 64) for m in range(2)]
    out_specs = [rows_of(128 + 64 * m, 64) for m in range(2)]
    project_spec = pl.BlockSpec((32, 64, WIDTH), lambda *at: (0, 4, 0))
    last_spec, first_spec, conv_spec = rows_of(304, 16), rows_of(320, 32), rows_of(352, 16)

    x1, hidden, query_u, query_v, key, value = call(
        feed_front,
        [x_spec, vec_spec, in_specs[0], out_specs[0], project_spec],
        [(FULL, F32), ((4,) + FULL, BF)] + [(FULL, BF)] * 4,
        [(FULL, BF), (FULL, F32)],
    )(frames, vec, weights, weights, weights)

    probs_spec = pl.BlockSpec((2, LEN, LEN), lambda h: (h, 0, 0))
    offsets_spec = pl.BlockSpec((2 * LEN, 128), lambda h: (0, h))
    probs, mixed, offsets = call(
        attend,
        [pair()] * 4 + [pl.BlockSpec((256, 128), lambda h: (0, h)), whole((2 * LEN, 1))],
        [((8, LEN, LEN), BF), (FULL, BF), ((2 * LEN, WIDTH), BF)],
        [((2 * LEN, 256), BF), (FULL, F32)],
        grid=(4,),
        out_specs=[probs_spec, pair(), offsets_spec],
    )(query_u, query_v, key, value, table, tall)

    x2, gates, gated, deep, stats = call(
        conv_front,
        [full, full, last_spec, first_spec, vec_spec],
        [(FULL, F32), ((2,) + FULL, BF), (FULL, BF), (FULL, F32), ((32, 8, 128), F32)],
        [((PADDED, WIDTH), F32)],
    )(mixed, x1, weights, weights, vec)
    stats = share(stats)

    y, gx3, before_grad, stats_back, grads4, sums4 = call(
        centre,
        [WHERE, full, stats_spec, full, conv_spec, in_specs[1], out_specs[1], vec_spec, cotangent_spec],
        [((TILE, WIDTH), BF), (FULL, F32), (FULL, F32), ((32, 8, 128), F32), ((32, 144, 128), BF), ((8, WIDTH), F32)],
        [(FULL, BF), ((4,) + FULL, BF), (FULL, F32), (FULL, BF), (FULL, BF), (FULL, F32)],
    )(where, deep, stats, x2, weights, weights, weights, vec, frames)
    stats_back = share(stats_back)

    gx2, mixed_grad, grads5, sums5 = call(
        conv_back,
        [WHERE, full, stats_spec, stats_spec, full, full, whole((2,) + FULL), full, full, first_spec, last_spec, full, vec_spec],
        [(FULL, F32), (FULL, BF), ((32, 48, 128), BF), ((40, WIDTH), F32)],
        [((PADDED, WIDTH), F32), ((PADDED, WIDTH), F32), (FULL, F32), ((KERNEL, 8, WIDTH), F32), ((LEN, 2 * WIDTH), BF), (FULL, BF)],
    )(where, before_grad, stats_back, stats, deep, gated, gates, x2, gx3, weights, weights, mixed, vec)

    query_grad, key_grad, value_grad, sums6, grads6 = call(
        attend_back,
        [WHERE] + [pair()] * 5 + [probs_spec, offsets_spec, whole((1, 2 * LEN))],
        [(FULL, BF)] * 3 + [((8, WIDTH), F32), ((32, 16, 128), BF)],
        [(FULL, BF), ((LEN, 128), F32), ((LEN, 128), F32), ((2 * LEN, 128), F32)],
        grid=(4,),
        out_specs=[pair()] * 3 + [pl.BlockSpec((8, 128), lambda h: (0, h)), whole((32, 16, 128))],
    )(where, query_u, query_v, key, value, mixed_grad, probs, offsets, long)

    gx0, grads7 = call(
        feed_last,
        [WHERE] + [full] * 5 + [project_spec, in_specs[0], out_specs[0], whole((4,) + FULL), x_spec, vec_spec]
        + [whole((8, WIDTH)), whole((40, WIDTH)), whole((8, WIDTH))],
        [((TILE, WIDTH), F32), ((32, 192, 128), BF)],
        [((LEN, 3 * WIDTH), BF), (FULL, BF), (FULL, F32), (FULL, BF), (FULL, BF), (FULL, F32), ((128, WIDTH), F32)],
    )(where, query_grad, key_grad, value_grad, x1, gx2, weights, weights, weights, hidden, frames, vec, sums4, sums5, sums6)

    grads = jnp.concatenate([grads4, grads5, grads6, grads7], axis=1).reshape(16, 2, 400, 128)
    core = lax.axis_index("c")
    sent = lax.dynamic_index_in_dim(grads, 1 - core, axis=1, keepdims=False)
    kept = lax.dynamic_index_in_dim(grads, core, axis=1, keepdims=False)
    other = lax.ppermute(sent, "c", [(0, 1), (1, 0)])
    chip = (kept.astype(F32) + other.astype(F32)).astype(BF)
    chip = lax.all_to_all(chip, ("y", "z"), 0, 0, tiled=True)
    summed = jnp.sum(chip.astype(F32), axis=0).astype(BF)
    parts = lax.all_gather(summed, "x", axis=0, tiled=False)
    results = call(
        unpack,
        [whole((4, 400, 128))],
        [((2, 16, 2048), F32), ((2, 64, 512), F32), ((16, 1536), F32), ((16, 512), F32), ((8, 512), F32),
         ((16, 1024), F32), ((KERNEL, 16), F32), ((16, 512), F32), ((6, 16), F32), ((8, 16), F32)],
        [],
    )(parts)
    return (y[None], gx0[None]) + tuple(result[None] for result in results)


def solution(mesh):
    fine = Mesh(mesh.devices.reshape(4, 4, 2, 4), ("y", "z", "c", "x"))
    fsdp = ("y", "z", "c")
    activations = P(fsdp, "x", None)
    placed = (
        activations,
        P(None, None, fsdp, None),
        P(None, None, fsdp, None),
        P(None, fsdp, None),
        P(None, fsdp, None),
        P(None, fsdp, None),
        P(None, fsdp, None),
        P(None, None, fsdp),
        P(None, fsdp, None),
        P(None, None, fsdp),
        P(None, None, fsdp),
    )
    return jax.shard_map(
        shards,
        mesh=fine,
        in_specs=placed + (P(), activations),
        out_specs=(activations, activations) + placed[1:],
        check_vma=False,
    )
```

```python
import functools

import jax
import jax.numpy as jnp
from jax import lax
from jax.experimental import pallas as pl
from jax.experimental.pallas import tpu as pltpu
from jax.sharding import Mesh
from jax.sharding import PartitionSpec as P

EPSILON = 1e-05
KERNEL = 31
LEN = 512
WIDTH = 512
CHUNKS = 4
TILE = 128
SPAN = TILE + LEN
FRAMES = 16384
BF = jnp.bfloat16
F32 = jnp.float32
GAIN, SHIFT, TAP = 0, 6, 14
FRONT = 16
PADDED = 560


def dot(left, right):
    return lax.dot_general(left, right, (((1,), (0,)), ((), ())), preferred_element_type=F32)


def dot_right(left, right):
    return lax.dot_general(left, right, (((1,), (1,)), ((), ())), preferred_element_type=F32)


def dot_left(left, right):
    return lax.dot_general(left, right, (((0,), (0,)), ((), ())), preferred_element_type=F32)


def normalise(values):
    centred = values - jnp.mean(values, axis=-1, keepdims=True)
    inverse_root = lax.rsqrt(jnp.mean(centred * centred, axis=-1, keepdims=True) + EPSILON)
    return centred * inverse_root, inverse_root


def norm_back(upstream, normed, inverse_root, gain):
    scaled = upstream * gain
    inner = (
        scaled
        - jnp.mean(scaled, axis=-1, keepdims=True)
        - normed * jnp.mean(scaled * normed, axis=-1, keepdims=True)
    )
    return inverse_root * inner


def sigmoid(values):
    return 0.5 * jnp.tanh(0.5 * values) + 0.5


def column_sum(values):
    return jnp.sum(values, axis=0, keepdims=True)


def row(vec, index):
    return vec[index : index + 1, :]


def flat(block):
    return block.reshape(block.shape[0] * block.shape[1], block.shape[2])


def divide(core, kept, sent, at, block):
    block = block.reshape(block.shape[0] // 2, 2, block.shape[1], 128).astype(BF)
    first, second = block[:, 0], block[:, 1]
    kept[at] = jnp.where(core == 0, first, second)
    sent[at] = jnp.where(core == 0, second, first)


def pieces(core, kept, sent, first, grad):
    for lane in range(grad.shape[1] // 128):
        part = grad[:, lane * 128 : (lane + 1) * 128]
        high = part.shape[0] // 32
        at = (slice(None), slice(first + lane * high, first + lane * high + high))
        divide(core, kept, sent, at, part.reshape(32, high, 128))


def lanes(ref, start, size):
    return ref[:, pl.ds(pl.multiple_of(start, 128), size)]


def spread(out, sums):
    for which in range(2):
        for lane in range(4):
            line = sums[which][:, lane * 128 : (lane + 1) * 128]
            out[:, 4 * which + lane, :] = jnp.broadcast_to(line, (32, 128))


def collect(stats):
    total = jnp.sum(stats[...], axis=0)
    return [
        jnp.concatenate([total[4 * which + lane : 4 * which + lane + 1] for lane in range(4)], axis=1)
        for which in range(2)
    ]


def pack(m_in, m_out, project, last, table, first, taps, conv, gain, shift, out, small):
    for m in range(2):
        for j in range(4):
            at = 64 * m + 16 * j
            out[at : at + 16, :] = m_in[0, m, :, 512 * j : 512 * j + 512]
        out[128 + 64 * m : 192 + 64 * m, :] = m_out[0, m]
    for j in range(3):
        out[256 + 16 * j : 272 + 16 * j, :] = project[0, :, 512 * j : 512 * j + 512]
    out[304:320, :] = last[0]
    for j in range(2):
        out[320 + 16 * j : 336 + 16 * j, :] = first[0, :, 512 * j : 512 * j + 512]
    out[352:368, :] = conv[0]
    table_rows = table[0].astype(F32)
    out[368:384, :] = jnp.concatenate([table_rows, jnp.zeros_like(table_rows)], axis=0).astype(BF)
    small[...] = jnp.zeros_like(small)
    small[GAIN : GAIN + 6, :] = gain[0].astype(F32)
    small[SHIFT : SHIFT + 8, :] = shift[0].astype(F32)
    small[TAP : TAP + KERNEL, :] = taps[...].astype(F32).T
    out[384:400, :] = jnp.zeros((16, WIDTH), BF)
    out[384:400, 0:128] = small[...].T.astype(BF)


def feed_front(x, small, matrix_in, matrix_out, project, x1, hidden, query_u, query_v, key, value, vec, fed, total, wait):
    wait(0, 1)
    vec[...] = flat(small[...]).astype(F32).T
    values = x[...].astype(F32)
    normed, _ = normalise(values)
    fed[...] = (normed * row(vec, GAIN) + row(vec, SHIFT)).astype(BF)
    wait(2, 3)
    for j in range(CHUNKS):
        part = dot(fed[...], flat(matrix_in[:, 16 * j : 16 * j + 16, :]))
        hidden[j] = part.astype(BF)
        active = (part * sigmoid(part)).astype(BF)
        grown = dot(active, flat(matrix_out[8 * j : 8 * j + 8]))
        total[...] = grown if j == 0 else total[...] + grown
    after = values + 0.5 * total[...]
    x1[...] = after
    normed, _ = normalise(after)
    fed[...] = (normed * row(vec, GAIN + 1) + row(vec, SHIFT + 1)).astype(BF)
    wait(4)
    query = dot(fed[...], flat(project[:, 0:16, :]))
    query_u[...] = ((query + row(vec, SHIFT + 6)) * 0.125).astype(BF)
    query_v[...] = ((query + row(vec, SHIFT + 7)) * 0.125).astype(BF)
    key[...] = dot(fed[...], flat(project[:, 16:32, :])).astype(BF)
    value[...] = dot(fed[...], flat(project[:, 32:48, :])).astype(BF)


def head_mask(which, rows):
    lane = lax.broadcasted_iota(jnp.int32, (rows, 128), 1)
    return (lane < 64) if which == 0 else (lane >= 64)


def mirror_tile():
    row_at = lax.broadcasted_iota(jnp.int32, (TILE, TILE), 0)
    column_at = lax.broadcasted_iota(jnp.int32, (TILE, TILE), 1)
    return (row_at + column_at == TILE - 1).astype(F32).astype(BF)


def both_heads(block):
    halves = [jnp.where(head_mask(head, TILE), block, 0.0).astype(BF) for head in range(2)]
    return jnp.concatenate(halves, axis=0)


def attend(query_u, query_v, key, value, table, bucket, probs, mixed, offsets, chosen):
    number = lax.broadcasted_iota(jnp.int32, (2 * LEN, 256), 1)
    chosen[...] = (bucket[...] == number).astype(F32).astype(BF)
    mirror = mirror_tile()

    def step(pair, carry):
        lane = pl.ds(pl.multiple_of(pair * 128, 128), 128)
        table_rows = table[:, :, lane].astype(F32)[:, 0:8, :].reshape(256, 128).astype(BF)
        offsets[:, lane] = dot(chosen[...], table_rows).astype(BF)
        for t in range(4):
            rows = slice(t * TILE, (t + 1) * TILE)
            start = LEN - TILE - TILE * t
            content, place = both_heads(query_u[rows, lane]), both_heads(query_v[rows, lane])
            relative = dot_right(place, offsets[start : start + SPAN, lane])
            scores = dot_right(content, key[:, lane])
            lows = []
            for head in range(2):
                part = slice(head * TILE, head * TILE + TILE)
                placed = pltpu.roll(relative[part], SPAN - TILE + 1, 1, stride=1, stride_axis=0)
                logits = scores[part] + placed[:, :LEN]
                expo = jnp.exp(logits - jnp.max(logits, axis=1, keepdims=True))
                lows.append((expo * (1.0 / jnp.sum(expo, axis=1, keepdims=True))).astype(BF))
                probs[2 * pair + head, rows, :] = dot(mirror, lows[head]).astype(BF)
            outs = dot(jnp.concatenate(lows, axis=0), value[:, lane])
            mixed[rows, lane] = jnp.where(head_mask(0, TILE), outs[:TILE], outs[TILE:]).astype(BF)
        return carry

    lax.fori_loop(0, 4, step, 0)


def depthwise(padded, vec, out, flip):
    def step(index, carry):
        lane = pl.multiple_of((index % 4) * 128, 128)
        first = pl.multiple_of((index // 4) * 64, 64)
        window = padded[pl.ds(first, 96), pl.ds(lane, 128)]
        total = None
        for shift in range(8):
            part = None
            for q in range(4):
                tap = 8 * q + shift - 1
                if tap < 0 or tap >= KERNEL:
                    continue
                tap = KERNEL - 1 - tap if flip else tap
                term = window[8 * q : 8 * q + 72] * vec[TAP + tap : TAP + tap + 1, pl.ds(lane, 128)]
                part = term if part is None else part + term
            part = part[shift : shift + 64]
            total = part if total is None else total + part
        out[pl.ds(first, 64), pl.ds(lane, 128)] = total
        return carry

    lax.fori_loop(0, 32, step, 0)


def fill(padded, values):
    padded[0:FRONT, :] = jnp.zeros((FRONT, WIDTH), F32)
    padded[FRONT : FRONT + LEN, :] = values
    padded[FRONT + LEN :, :] = jnp.zeros((PADDED - FRONT - LEN, WIDTH), F32)


def conv_front(mixed, x1, project, first, vec, x2, gates, gated, deep, stats, padded, wait, send):
    wait(6)
    after = x1[...] + dot(mixed[...], flat(project[...]))
    x2[...] = after
    normed, _ = normalise(after)
    conv_in = (normed * row(vec, GAIN + 2) + row(vec, SHIFT + 2)).astype(BF)
    wait(7)
    half = dot(conv_in, flat(first[:, 0:16, :]))
    gate = dot(conv_in, flat(first[:, 16:32, :]))
    gates[0] = half.astype(BF)
    gates[1] = gate.astype(BF)
    low = (half * sigmoid(gate)).astype(BF)
    gated[...] = low
    send(10, 11, 12)
    fill(padded, low.astype(F32))
    depthwise(padded, vec, deep, False)
    send(13)
    values = deep[...]
    spread(stats, (column_sum(values), column_sum(values * values)))


def begin(sources, targets, semaphores):
    copies = [
        pltpu.make_async_copy(source, target, semaphores.at[index])
        for index, (source, target) in enumerate(zip(sources, targets))
    ]
    for copy in copies:
        copy.start()

    def wait(*which):
        for index in which:
            copies[index].wait()

    return wait


def front(
    bucket, frames, weights,
    x1_out, hidden_out, u_out, v_out, key_out, value_out, vec_out, probs_out, mixed_out, offsets_out,
    x2_out, gates_out, gated_out, deep_out, stats,
    x, small, matrix_in, matrix_out, project, table, last, first,
    x1, hidden, query_u, query_v, key, value, vec, probs, mixed, offsets, x2, gates, gated, deep,
    fed, total, chosen, padded, arrived, left,
):
    wait = begin(
        [frames, weights.at[:, 384:400, 0:128]]
        + [weights.at[:, at : at + size, :] for at, size in ((0, 64), (128, 64), (256, 48), (368, 16), (304, 16), (320, 32))],
        [x, small, matrix_in, matrix_out, project, table, last, first],
        arrived,
    )
    held = [x1, hidden, query_u, query_v, key, value, vec, probs, mixed, offsets, x2, gates, gated, deep]
    outs = [
        x1_out, hidden_out, u_out, v_out, key_out, value_out, vec_out, probs_out, mixed_out, offsets_out,
        x2_out, gates_out, gated_out, deep_out,
    ]
    sent = [
        pltpu.make_async_copy(source, target, left.at[index])
        for index, (source, target) in enumerate(zip(held, outs))
    ]

    def send(*which):
        for index in which:
            sent[index].start()

    feed_front(x, small, matrix_in, matrix_out, project, x1, hidden, query_u, query_v, key, value, vec, fed, total, wait)
    send(0, 1, 2, 3, 4, 5, 6)
    wait(5)
    attend(query_u, query_v, key, value, table, bucket, probs, mixed, offsets, chosen)
    send(7, 8, 9)
    conv_front(mixed, x1, last, first, vec, x2, gates, gated, deep, stats, padded, wait, send)
    for copy in sent:
        copy.wait()


def batch_norm(stats, deep, vec):
    total, square = collect(stats)
    average = total / FRAMES
    inverse_root = lax.rsqrt(square / FRAMES - average * average + EPSILON)
    return (deep - average) * inverse_root, inverse_root


def feed_back(upstream, fed, hidden, matrix_in, matrix_out, kept, sent, u_low, grown, total, quarter, core):
    u_low[...] = upstream.astype(BF)
    side = lanes(u_low, quarter * 128, 128)
    for j in range(CHUNKS):
        part = hidden[j].astype(F32)
        logistic = sigmoid(part)
        active = (part * logistic).astype(BF)
        out_grad = dot_left(active, side)
        at = (slice(4 * j, 4 * j + 4), slice(64, 128))
        divide(core, kept, sent, at, out_grad.reshape(8, 64, 128))
        slope = logistic * (1.0 + part * (1.0 - logistic))
        grown[...] = (dot_right(u_low[...], flat(matrix_out[8 * j : 8 * j + 8])) * slope).astype(BF)

        @pl.when(quarter == j)
        def _():
            pieces(core, kept, sent, 0, dot_left(fed[...], grown[...]))

        back = dot_right(grown[...], flat(matrix_in[:, 16 * j : 16 * j + 16, :]))
        total[...] = back if j == 0 else total[...] + back


def centre(
    where, stats, deep_in, vec_in, x2_in, weights, cotangent_in,
    gx3_out, before_grad_out, y, stats_back, kept, sent, sums,
    deep, vec, x2, last, matrix_in, matrix_out, cotangent, gx3, before_grad,
    fed, hidden, total, u_low, grown, wide, arrived, left,
):
    wait = begin(
        [deep_in, vec_in, weights.at[:, 352:368, :], x2_in, weights.at[:, 64:128, :], weights.at[:, 192:256, :], cotangent_in],
        [deep, vec, last, x2, matrix_in, matrix_out, cotangent],
        arrived,
    )
    wait(0, 1)
    quarter, core = where[0], where[1]
    own = pl.ds(pl.multiple_of(quarter * TILE, TILE), TILE)
    centred, _ = batch_norm(stats, deep[...], vec)
    before = centred * row(vec, GAIN + 5) + row(vec, SHIFT + 5)
    swish = (before * sigmoid(before)).astype(BF)
    wait(2, 3)
    x3 = x2[...] + dot(swish, flat(last[...]))
    wide[...] = x3
    normed, inverse_root = normalise(x3)
    fed[...] = (normed * row(vec, GAIN + 3) + row(vec, SHIFT + 3)).astype(BF)
    wait(4, 5)
    for j in range(CHUNKS):
        part = dot(fed[...], flat(matrix_in[:, 16 * j : 16 * j + 16, :]))
        hidden[j] = part.astype(BF)
        active = (part * sigmoid(part)).astype(BF)
        out = dot(active, flat(matrix_out[8 * j : 8 * j + 8]))
        total[...] = out if j == 0 else total[...] + out
    x4 = wide[...] + 0.5 * total[...]
    normed4, inverse4 = normalise(x4)
    gx3[...] = normed4 * row(vec, GAIN + 4) + row(vec, SHIFT + 4)
    y[...] = gx3[own, :].astype(BF)
    wait(6)
    upstream = cotangent[...].astype(F32)
    sums[...] = jnp.zeros_like(sums)
    sums[2:3, :] = column_sum(upstream * normed4)
    sums[3:4, :] = column_sum(upstream)
    gx4 = norm_back(upstream, normed4, inverse4, row(vec, GAIN + 4))
    gx3[...] = gx4
    feed_back(0.5 * gx4, fed, hidden, matrix_in, matrix_out, kept, sent, u_low, grown, total, quarter, core)
    upstream = total[...]
    normed, inverse_root = normalise(wide[...])
    sums[0:1, :] = column_sum(upstream * normed)
    sums[1:2, :] = column_sum(upstream)
    after = gx3[...] + norm_back(upstream, normed, inverse_root, row(vec, GAIN + 3))
    gx3[...] = after
    gx3_sent = pltpu.make_async_copy(gx3, gx3_out, left.at[0])
    gx3_sent.start()
    u_low[...] = after.astype(BF)
    centred, _ = batch_norm(stats, deep[...], vec)
    before = centred * row(vec, GAIN + 5) + row(vec, SHIFT + 5)
    logistic = sigmoid(before)
    swish = (before * logistic).astype(BF)
    pieces(core, kept, sent, 128, dot_left(swish, lanes(u_low, quarter * 128, 128)))
    slope = logistic * (1.0 + before * (1.0 - logistic))
    back = dot_right(u_low[...], flat(last[...])) * slope
    before_grad[...] = back
    back_sent = pltpu.make_async_copy(before_grad, before_grad_out, left.at[1])
    back_sent.start()
    shift_sum, gain_sum = column_sum(back), column_sum(back * centred)
    sums[4:5, :] = gain_sum
    sums[5:6, :] = shift_sum
    spread(stats_back, (shift_sum, gain_sum))
    gx3_sent.wait()
    back_sent.wait()


def tap_grads(padded, padded_grad, acc):
    acc[...] = jnp.zeros_like(acc)

    def step(index, carry):
        lane = pl.multiple_of((index % 4) * 128, 128)
        first = pl.multiple_of((index // 4) * 104, 8)
        grad = padded_grad[pl.ds(first + 8, 112), pl.ds(lane, 128)]
        window = padded[pl.ds(first, 128), pl.ds(lane, 128)]
        for shift in range(8):
            moved = grad[8 - shift : 112 - shift]
            for q in range(4):
                tap = 8 * q + shift - 1
                if tap < 0 or tap >= KERNEL:
                    continue
                term = (window[8 * q : 8 * q + 104] * moved).reshape(13, 8, 128)
                acc[tap, :, pl.ds(lane, 128)] += jnp.sum(term, axis=0)
        return carry

    lax.fori_loop(0, 20, step, 0)


def conv_back(
    quarter, core, wait, before_grad, stats_back, stats, deep, gated, gates, x2, gx3, first, project, mixed, vec,
    gx2, mixed_grad, kept, sent, packed,
    padded, padded_grad, total, acc, both, u_low,
):
    wait(0, 1, 2)
    centred, inverse_root = batch_norm(stats, deep[...], vec)
    shift_sum, gain_sum = collect(stats_back)
    inner = before_grad[...] - shift_sum / FRAMES - centred * (gain_sum / FRAMES)
    low = (inverse_root * row(vec, GAIN + 5) * inner).astype(BF)
    fill(padded_grad, low.astype(F32))
    wait(3)
    fill(padded, gated[...].astype(F32))
    depthwise(padded_grad, vec, total, True)
    tap_grads(padded, padded_grad, acc)
    for tap in range(KERNEL):
        packed[TAP + tap : TAP + tap + 1, :] = column_sum(acc[tap])
    wait(4, 5, 6, 7, 8, 9)
    opened = sigmoid(gates[1].astype(F32))
    passed = total[...] * opened
    both[:, 0:WIDTH] = passed.astype(BF)
    both[:, WIDTH:] = (passed * gates[0].astype(F32) * (1.0 - opened)).astype(BF)
    normed, inverse_root = normalise(x2[...])
    conv_in = (normed * row(vec, GAIN + 2) + row(vec, SHIFT + 2)).astype(BF)
    pieces(core, kept, sent, 192, dot_left(conv_in, lanes(both, quarter * 256, 256)))
    upstream = dot_right(both[:, 0:WIDTH], flat(first[:, 0:16, :]))
    upstream = upstream + dot_right(both[:, WIDTH:], flat(first[:, 16:32, :]))
    packed[GAIN + 2 : GAIN + 3, :] = column_sum(upstream * normed)
    packed[SHIFT + 2 : SHIFT + 3, :] = column_sum(upstream)
    after = gx3[...] + norm_back(upstream, normed, inverse_root, row(vec, GAIN + 2))
    gx2[...] = after
    u_low[...] = after.astype(BF)
    pieces(core, kept, sent, 224, dot_left(mixed[...], lanes(u_low, quarter * 128, 128)))
    mixed_grad[...] = dot_right(u_low[...], flat(project[...])).astype(BF)


def attend_back(
    quarter, core, query_u, query_v, key, value, mixed_grad, probs, offsets, bucket,
    three, packed, kept, sent,
    score_grad, turned, u_side, v_side, g_side, key_side, value_side, offset_grad,
):
    mirror = mirror_tile()
    left_tile = head_mask(0, TILE)

    def step(pair, carry):
        mine = quarter == pair

        def lane_at(base):
            return pl.ds(pl.multiple_of(base + pair * 128, 128), 128)

        lane = lane_at(0)
        for t in range(4):
            rows = slice(t * TILE, (t + 1) * TILE)
            turned[rows, :] = dot(mirror, mixed_grad[rows, lane]).astype(BF)
            u_side[:, rows] = dot_left(query_u[rows, lane], mirror).astype(BF)
            v_side[:, rows] = dot_left(query_v[rows, lane], mirror).astype(BF)
            g_side[:, rows] = dot_left(mixed_grad[rows, lane], mirror).astype(BF)

        @pl.when(mine)
        def _():
            offset_grad[...] = jnp.zeros_like(offset_grad)

        from_u, from_v = [], []
        for t in range(4):
            rows = slice(t * TILE, (t + 1) * TILE)
            start = LEN - TILE - TILE * t
            window = slice(start, start + SPAN)
            prob_grads = dot_right(both_heads(turned[rows, :]), value[:, lane])
            lows, placed = [], []
            for head in range(2):
                part = slice(head * TILE, head * TILE + TILE)
                chance = probs[2 * pair + head, rows, :].astype(F32)
                weighed = chance * prob_grads[part]
                grad = weighed - chance * jnp.sum(weighed, axis=1, keepdims=True)
                low = grad.astype(BF)
                score_grad[head, rows, :] = low
                lows.append(low)
                padded = jnp.concatenate([grad, jnp.zeros((TILE, TILE), F32)], axis=1)
                placed.append(pltpu.roll(padded, 0, 1, stride=1, stride_axis=0).astype(BF))
            u_parts = dot(jnp.concatenate(lows, axis=0), key[:, lane])
            v_parts = dot(jnp.concatenate(placed, axis=0), offsets[window, lane])

            @pl.when(mine)
            def _():
                for head in range(2):
                    side = slice(64 * head, 64 * head + 64)
                    offset_grad[side, window] += dot(v_side[side, rows], placed[head])

            u_part = jnp.where(left_tile, u_parts[:TILE], u_parts[TILE:]) * 0.125
            v_part = jnp.where(left_tile, v_parts[:TILE], v_parts[TILE:]) * 0.125
            from_u.append(column_sum(u_part))
            from_v.append(column_sum(v_part))
            three[rows, lane] = dot(mirror, (u_part + v_part).astype(BF)).astype(BF)
        for head in range(2):
            side = slice(64 * head, 64 * head + 64)
            key_side[side, :] = dot(u_side[side, :], score_grad[head])
            value_side[side, :] = dot(g_side[side, :], probs[2 * pair + head])
        three[:, lane_at(WIDTH)] = key_side[...].T.astype(BF)
        three[:, lane_at(2 * WIDTH)] = value_side[...].T.astype(BF)
        packed[SHIFT + 6 : SHIFT + 7, lane] = from_u[0] + from_u[1] + from_u[2] + from_u[3]
        packed[SHIFT + 7 : SHIFT + 8, lane] = from_v[0] + from_v[1] + from_v[2] + from_v[3]

        @pl.when(mine)
        def _():
            number = lax.broadcasted_iota(jnp.int32, (2 * LEN, 256), 1)
            chosen = (bucket[...] == number).astype(F32).astype(BF)
            table_grad = dot(offset_grad[...].astype(BF), chosen).T.reshape(32, 8, 128)
            table_grad = jnp.concatenate([table_grad, jnp.zeros((32, 8, 128), F32)], axis=1)
            divide(core, kept, sent, (slice(None), slice(240, 256)), table_grad)

        return carry

    lax.fori_loop(0, 4, step, 0)


def feed_last(
    quarter, core, wait, x1, gx2, project, matrix_in, matrix_out, hidden, x, vec, sums4,
    gx0, kept, sent,
    three, fed, total, u_low, grown, wide, packed,
):
    own = pl.ds(pl.multiple_of(quarter * TILE, TILE), TILE)
    wait(15, 16, 17, 18, 19, 20)
    normed, inverse_root = normalise(x1[...])
    attn_in = (normed * row(vec, GAIN + 1) + row(vec, SHIFT + 1)).astype(BF)
    pieces(core, kept, sent, 128, dot_left(attn_in, lanes(three, quarter * 384, 384)))
    upstream = dot_right(three[:, 0:WIDTH], flat(project[:, 0:16, :]))
    upstream = upstream + dot_right(three[:, WIDTH : 2 * WIDTH], flat(project[:, 16:32, :]))
    upstream = upstream + dot_right(three[:, 2 * WIDTH :], flat(project[:, 32:48, :]))
    packed[GAIN + 1 : GAIN + 2, :] = column_sum(upstream * normed)
    packed[SHIFT + 1 : SHIFT + 2, :] = column_sum(upstream)
    gx1 = gx2[...] + norm_back(upstream, normed, inverse_root, row(vec, GAIN + 1))
    wide[...] = gx1
    normed, inverse_root = normalise(x[...].astype(F32))
    fed[...] = (normed * row(vec, GAIN) + row(vec, SHIFT)).astype(BF)
    feed_back(0.5 * gx1, fed, hidden, matrix_in, matrix_out, kept, sent, u_low, grown, total, quarter, core)
    upstream = total[...]
    normed, inverse_root = normalise(x[...].astype(F32))
    packed[GAIN : GAIN + 1, :] = column_sum(upstream * normed)
    packed[SHIFT : SHIFT + 1, :] = column_sum(upstream)
    wide[...] = wide[...] + norm_back(upstream, normed, inverse_root, row(vec, GAIN))
    gx0[...] = wide[own, :]
    for index in range(3):
        packed[GAIN + 3 + index : GAIN + 4 + index, :] = row(sums4, 2 * index)
        packed[SHIFT + 3 + index : SHIFT + 4 + index, :] = row(sums4, 2 * index + 1)
    pieces(core, kept, sent, 176, packed[...].T)


def back(
    where, bucket, stats_back, stats, sums4,
    before_in, deep_in, vec_in, gated_in, gates_in, x2_in, weights, gx3_in, mixed_in,
    u_in, v_in, key_in, value_in, probs_in, offsets_in, x1_in, hidden_in, frames,
    gx0, kept, sent,
    before_grad, deep, vec, gated, gates, x2, first, gx3, last, mixed,
    query_u, query_v, key, value, probs, offsets, x1, project, matrix_in, matrix_out, hidden, x,
    gx2, mixed_grad, packed, padded, padded_grad, total, acc, both, u_low,
    three, score_grad, turned, u_side, v_side, g_side, key_side, value_side, offset_grad,
    fed, grown, wide, arrived,
):
    quarter, core = where[0], where[1]

    def part(at, size):
        return weights.at[:, at : at + size, :]

    wait = begin(
        [before_in, deep_in, vec_in, gated_in, gates_in, x2_in, part(320, 32), gx3_in, part(304, 16), mixed_in]
        + [value_in, probs_in, key_in, offsets_in, u_in]
        + [x1_in, part(256, 48), part(0, 64), part(128, 64), hidden_in, frames, v_in],
        [before_grad, deep, vec, gated, gates, x2, first, gx3, last, mixed]
        + [value, probs, key, offsets, query_u]
        + [x1, project, matrix_in, matrix_out, hidden, x, query_v],
        arrived,
    )
    packed[...] = jnp.zeros_like(packed)
    conv_back(
        quarter, core, wait, before_grad, stats_back, stats, deep, gated, gates, x2, gx3, first, last, mixed, vec,
        gx2, mixed_grad, kept, sent, packed,
        padded, padded_grad, total, acc, both, u_low,
    )
    wait(10, 11, 12, 13, 14, 21)
    attend_back(
        quarter, core, query_u, query_v, key, value, mixed_grad, probs, offsets, bucket,
        three, packed, kept, sent,
        score_grad, turned, u_side, v_side, g_side, key_side, value_side, offset_grad,
    )
    feed_last(
        quarter, core, wait, x1, gx2, project, matrix_in, matrix_out, hidden, x, vec, sums4,
        gx0, kept, sent,
        three, fed, total, u_low, grown, wide, packed,
    )


def unpack(
    where, part0, part1, part2, part3,
    g_in, g_out, g_project, g_last, g_table, g_first, g_taps, g_conv, g_gain, g_shift,
):
    for hop, part in enumerate((part0, part1, part2, part3)):
        side = lax.rem(where[0] + 4 - hop, 4)

        def put(out, first, rows, wide, lane, m=None, part=part, side=side):
            at = pl.ds(pl.multiple_of(side * wide + lane * 128, 128), 128)
            block = part[first : first + rows, :].astype(F32)
            if m is None:
                out[:, at] = block[0 : out.shape[0]]
            else:
                out[m, :, at] = block

        for m, base in ((0, 0), (1, 256)):
            for lane in range(4):
                put(g_in, base + 16 * lane, 16, 512, lane, m)
            put(g_out, base + 64, 64, 128, 0, m)
        for lane in range(3):
            put(g_project, 128 + 16 * lane, 16, 384, lane)
        for lane in range(2):
            put(g_first, 192 + 16 * lane, 16, 256, lane)
        put(g_last, 224, 16, 128, 0)
        put(g_conv, 384, 16, 128, 0)
        put(g_table, 240, 16, 128, 0)
    vectors = part0[176:192, :].astype(F32)
    g_taps[...] = vectors[:, TAP : TAP + KERNEL]
    vectors = vectors.T
    for index in range(6):
        g_gain[index] = row(vectors, GAIN + index)
    g_shift[...] = vectors[SHIFT : SHIFT + 8]


def whole(shape):
    return pl.BlockSpec(shape, lambda *at: (0,) * len(shape), pipeline_mode=pl.Buffered(1))


WHERE = pl.BlockSpec(memory_space=pltpu.SMEM)
FULL = (LEN, WIDTH)
LIMIT = 56 << 20


ANYWHERE = pl.BlockSpec(memory_space=pl.ANY)


def call(kernel, micros, in_specs, outs, scratch, far=0, semaphores=()):
    return pl.pallas_call(
        kernel,
        grid=(1,),
        in_specs=in_specs,
        out_specs=[ANYWHERE if at < far else whole(shape) for at, (shape, _) in enumerate(outs)],
        out_shape=[jax.ShapeDtypeStruct(shape, dtype) for shape, dtype in outs],
        scratch_shapes=[pltpu.VMEM(shape, dtype) for shape, dtype in scratch]
        + [pltpu.SemaphoreType.DMA((count,)) for count in semaphores],
        compiler_params=pltpu.CompilerParams(vmem_limit_bytes=LIMIT),
        cost_estimate=pl.CostEstimate(flops=micros * 1150 * 10**6, bytes_accessed=0, transcendentals=0),
    )


def share(stats):
    return lax.all_to_all(stats, ("y", "z", "c"), 0, 0, tiled=True)


def with_core(kept, sent):
    other = lax.ppermute(sent, "c", [(0, 1), (1, 0)])
    return (kept.astype(F32) + other.astype(F32)).astype(BF)


def across(chip):
    return lax.all_to_all(chip, ("y", "z"), 0, 0, tiled=True)


def total_of(chip):
    return jnp.sum(chip.astype(F32), axis=0).astype(BF)


def shards(
    inputs, matrices_in, matrices_out, project_in, project_out, pos_table, conv_first, depth_taps,
    conv_last, gain_rows, shift_rows, bucket, cotangent,
):
    fsdp = ("y", "z", "c")
    where = jnp.stack([lax.axis_index("x"), lax.axis_index("c")]).astype(jnp.int32)

    packed = call(
        pack,
        2,
        [whole(part.shape) for part in (matrices_in, matrices_out, project_in, project_out, pos_table, conv_first)]
        + [whole((16, KERNEL)), whole(conv_last.shape), whole(gain_rows.shape), whole(shift_rows.shape)],
        [((400, WIDTH), BF)],
        [((128, 16), F32)],
    )(
        matrices_in, matrices_out, project_in, project_out, pos_table, conv_first,
        jnp.transpose(depth_taps, (0, 2, 1))[0], conv_last, gain_rows, shift_rows,
    )[0]
    weights = lax.all_gather(packed, fsdp, axis=0, tiled=False)
    frames = lax.all_gather(inputs[0], "x", axis=0, tiled=True)
    upstream = lax.all_gather(cotangent[0], "x", axis=0, tiled=True)
    frames, upstream = lax.optimization_barrier((frames, upstream))
    reversed_bucket = jnp.concatenate([bucket[::-1], jnp.full((1,), -1, jnp.int32)])
    tall = reversed_bucket.reshape(2 * LEN, 1)

    full, low, stats_shape = (FULL, F32), (FULL, BF), ((32, 8, 128), F32)
    vec_shape, four = ((128, WIDTH), F32), ((4,) + FULL, BF)
    two, probs_shape, offsets_shape = ((2,) + FULL, BF), ((8, LEN, LEN), BF), ((2 * LEN, WIDTH), BF)
    tall_spec, stats_spec = whole((2 * LEN, 1)), whole((32, 8, 128))

    def rows_of(size):
        return ((32, size, WIDTH), BF)

    held = [full, four, low, low, low, low, vec_shape, probs_shape, low, offsets_shape, full, two, low, full]
    (
        x1, hidden, query_u, query_v, key, value, vec, probs, mixed, offsets, x2, gates, gated, deep, stats,
    ) = call(
        front,
        28,
        [tall_spec, ANYWHERE, ANYWHERE],
        held + [stats_shape],
        [low, ((32, 16, 128), BF), rows_of(64), rows_of(64), rows_of(48), rows_of(16), rows_of(16), rows_of(32)]
        + held
        + [low, full, ((2 * LEN, 256), BF), ((PADDED, WIDTH), F32)],
        far=14,
        semaphores=(8, 14),
    )(tall, frames, weights)
    stats = share(stats)

    gx3, before_grad, y, stats_back, kept4, sent4, sums4 = call(
        centre,
        12,
        [WHERE, stats_spec] + [ANYWHERE] * 5,
        [full, full, ((TILE, WIDTH), BF), stats_shape, ((16, 144, 128), BF), ((16, 144, 128), BF), ((8, WIDTH), F32)],
        [full, vec_shape, full, rows_of(16), rows_of(64), rows_of(64), low, full, full]
        + [low, four, full, low, low, full],
        far=2,
        semaphores=(7, 2),
    )(where, stats, deep, vec, x2, weights, upstream)
    stats_back = share(stats_back)

    gx0, kept, sent = call(
        back,
        42,
        [WHERE, tall_spec, stats_spec, stats_spec, whole((8, WIDTH))] + [ANYWHERE] * 18,
        [((TILE, WIDTH), F32), ((16, 256, 128), BF), ((16, 256, 128), BF)],
        [full, full, vec_shape, low, two, full, rows_of(32), full, rows_of(16), low]
        + [low, low, low, low, probs_shape, offsets_shape, full, rows_of(48), rows_of(64), rows_of(64), four, low]
        + [full, low, vec_shape, ((PADDED, WIDTH), F32), ((PADDED, WIDTH), F32), full, ((KERNEL, 8, WIDTH), F32)]
        + [((LEN, 2 * WIDTH), BF), low, ((LEN, 3 * WIDTH), BF), two, ((LEN, 128), BF)]
        + [((128, LEN), BF)] * 3 + [((128, LEN), F32)] * 2 + [((128, 2 * LEN), F32)]
        + [low, low, full],
        semaphores=(22,),
    )(
        where, tall, stats_back, stats, sums4,
        before_grad, deep, vec, gated, gates, x2, weights, gx3, mixed,
        query_u, query_v, key, value, probs, offsets, x1, hidden, frames,
    )
    chips = [with_core(kept, sent), with_core(kept4, sent4)]
    total = total_of(across(jnp.concatenate(chips, axis=1)))
    hops = [[(i, (i + hop) % 4) for i in range(4)] for hop in range(4)]
    parts = [total] + [lax.ppermute(total, "x", hops[hop]) for hop in (1, 2, 3)]
    results = call(
        unpack,
        2,
        [WHERE] + [whole(total.shape)] * 4,
        [((2, 16, 2048), F32), ((2, 64, 512), F32), ((16, 1536), F32), ((16, 512), F32), ((8, 512), F32),
         ((16, 1024), F32), ((16, KERNEL), F32), ((16, 512), F32), ((6, 1, 16), F32), ((8, 16), F32)],
        [],
    )(where, *parts)
    results = list(results)
    results[6] = results[6].T
    results[8] = results[8][:, 0]
    return (y[None], gx0[None]) + tuple(result[None] for result in results)


def solution(mesh):
    fine = Mesh(mesh.devices.reshape(4, 4, 2, 4), ("y", "z", "c", "x"))
    fsdp = ("y", "z", "c")
    activations = P(fsdp, "x", None)
    placed = (
        activations,
        P(None, None, fsdp, None),
        P(None, None, fsdp, None),
        P(None, fsdp, None),
        P(None, fsdp, None),
        P(None, fsdp, None),
        P(None, fsdp, None),
        P(None, None, fsdp),
        P(None, fsdp, None),
        P(None, None, fsdp),
        P(None, None, fsdp),
    )
    return jax.shard_map(
        shards,
        mesh=fine,
        in_specs=placed + (P(), activations),
        out_specs=(activations, activations) + placed[1:],
        check_vma=False,
    )
```

```python
import functools

import jax
import jax.numpy as jnp
from jax import lax
from jax.experimental import pallas as pl
from jax.experimental.pallas import tpu as pltpu
from jax.sharding import Mesh
from jax.sharding import PartitionSpec as P

EPSILON = 1e-05
KERNEL = 31
LEN = 512
WIDTH = 512
CHUNKS = 4
TILE = 128
SPAN = TILE + LEN
FRAMES = 16384
BF = jnp.bfloat16
F32 = jnp.float32
GAIN, SHIFT, TAP = 0, 6, 14
FRONT = 16
PADDED = 560


def dot(left, right):
    return lax.dot_general(left, right, (((1,), (0,)), ((), ())), preferred_element_type=F32)


def dot_right(left, right):
    return lax.dot_general(left, right, (((1,), (1,)), ((), ())), preferred_element_type=F32)


def dot_left(left, right):
    return lax.dot_general(left, right, (((0,), (0,)), ((), ())), preferred_element_type=F32)


def normalise(values):
    centred = values - jnp.mean(values, axis=-1, keepdims=True)
    inverse_root = lax.rsqrt(jnp.mean(centred * centred, axis=-1, keepdims=True) + EPSILON)
    return centred * inverse_root, inverse_root


def norm_back(upstream, normed, inverse_root, gain):
    scaled = upstream * gain
    inner = (
        scaled
        - jnp.mean(scaled, axis=-1, keepdims=True)
        - normed * jnp.mean(scaled * normed, axis=-1, keepdims=True)
    )
    return inverse_root * inner


def sigmoid(values):
    return 0.5 * jnp.tanh(0.5 * values) + 0.5


def column_sum(values):
    return jnp.sum(values, axis=0, keepdims=True)


def row(vec, index):
    return vec[index : index + 1, :]


def flat(block):
    return block.reshape(block.shape[0] * block.shape[1], block.shape[2])


def divide(core, kept, sent, at, block):
    block = block.reshape(block.shape[0] // 2, 2, block.shape[1], 128).astype(BF)
    first, second = block[:, 0], block[:, 1]
    kept[at] = jnp.where(core == 0, first, second)
    sent[at] = jnp.where(core == 0, second, first)


def pieces(core, kept, sent, first, grad):
    for lane in range(grad.shape[1] // 128):
        part = grad[:, lane * 128 : (lane + 1) * 128]
        high = part.shape[0] // 32
        at = (slice(None), slice(first + lane * high, first + lane * high + high))
        divide(core, kept, sent, at, part.reshape(32, high, 128))


def lanes(ref, start, size):
    return ref[:, pl.ds(pl.multiple_of(start, 128), size)]


def spread(out, sums):
    for which in range(2):
        for lane in range(4):
            line = sums[which][:, lane * 128 : (lane + 1) * 128]
            out[:, 4 * which + lane, :] = jnp.broadcast_to(line, (32, 128))


def collect(stats):
    total = jnp.sum(stats[...], axis=0)
    return [
        jnp.concatenate([total[4 * which + lane : 4 * which + lane + 1] for lane in range(4)], axis=1)
        for which in range(2)
    ]


def pack(m_in, m_out, project, last, table, first, taps, conv, gain, shift, out, small):
    for m in range(2):
        for j in range(4):
            at = 64 * m + 16 * j
            out[at : at + 16, :] = m_in[0, m, :, 512 * j : 512 * j + 512]
        out[128 + 64 * m : 192 + 64 * m, :] = m_out[0, m]
    for j in range(3):
        out[256 + 16 * j : 272 + 16 * j, :] = project[0, :, 512 * j : 512 * j + 512]
    out[304:320, :] = last[0]
    for j in range(2):
        out[320 + 16 * j : 336 + 16 * j, :] = first[0, :, 512 * j : 512 * j + 512]
    out[352:368, :] = conv[0]
    table_rows = table[0].astype(F32)
    out[368:384, :] = jnp.concatenate([table_rows, jnp.zeros_like(table_rows)], axis=0).astype(BF)
    small[...] = jnp.zeros_like(small)
    small[GAIN : GAIN + 6, :] = gain[0].astype(F32)
    small[SHIFT : SHIFT + 8, :] = shift[0].astype(F32)
    small[TAP : TAP + KERNEL, :] = taps[...].astype(F32).T
    out[384:400, :] = jnp.zeros((16, WIDTH), BF)
    out[384:400, 0:128] = small[...].T.astype(BF)


def chunk(j):
    return slice(512 * j, 512 * j + 512)


def forward_hidden(fed, matrix_in, hidden, broad):
    for j in range(CHUNKS):
        part = dot(fed[...], flat(matrix_in[:, :, chunk(j)]))
        hidden[j] = part.astype(BF)
        broad[:, chunk(j)] = (part * sigmoid(part)).astype(BF)


def feed_front(x, small, matrix_in, matrix_out, project, x1, hidden, query_u, query_v, key, value, vec, fed, broad, wait):
    wait(0, 1)
    vec[...] = flat(small[...]).astype(F32).T
    values = x[...].astype(F32)
    normed, _ = normalise(values)
    fed[...] = (normed * row(vec, GAIN) + row(vec, SHIFT)).astype(BF)
    wait(7, 8, 9, 10)
    forward_hidden(fed, matrix_in, hidden, broad)
    wait(2)
    after = values + 0.5 * dot(broad[...], flat(matrix_out[...]))
    x1[...] = after
    normed, _ = normalise(after)
    fed[...] = (normed * row(vec, GAIN + 1) + row(vec, SHIFT + 1)).astype(BF)
    wait(3)
    query = dot(fed[...], flat(project[:, 0:16, :]))
    query_u[...] = ((query + row(vec, SHIFT + 6)) * 0.125).astype(BF)
    query_v[...] = ((query + row(vec, SHIFT + 7)) * 0.125).astype(BF)
    key[...] = dot(fed[...], flat(project[:, 16:32, :])).astype(BF)
    value[...] = dot(fed[...], flat(project[:, 32:48, :])).astype(BF)


def head_mask(which, rows):
    lane = lax.broadcasted_iota(jnp.int32, (rows, 128), 1)
    return (lane < 64) if which == 0 else (lane >= 64)


def mirror_tile():
    row_at = lax.broadcasted_iota(jnp.int32, (TILE, TILE), 0)
    column_at = lax.broadcasted_iota(jnp.int32, (TILE, TILE), 1)
    return (row_at + column_at == TILE - 1).astype(F32).astype(BF)


def both_heads(block):
    halves = [jnp.where(head_mask(head, TILE), block, 0.0).astype(BF) for head in range(2)]
    return jnp.concatenate(halves, axis=0)


def attend(query_u, query_v, key, value, table, bucket, probs, mixed, offsets, inverse, chosen):
    number = lax.broadcasted_iota(jnp.int32, (2 * LEN, 256), 1)
    chosen[...] = (bucket[...] == number).astype(F32).astype(BF)
    mirror = mirror_tile()

    def step(pair, carry):
        lane = pl.ds(pl.multiple_of(pair * 128, 128), 128)
        table_rows = table[:, :, lane].astype(F32)[:, 0:8, :].reshape(256, 128).astype(BF)
        offsets[:, lane] = dot(chosen[...], table_rows).astype(BF)
        with_ones = jnp.concatenate([value[:, lane], jnp.ones((LEN, 128), BF)], axis=1)
        for t in range(4):
            rows = slice(t * TILE, (t + 1) * TILE)
            start = LEN - TILE - TILE * t
            content, place = both_heads(query_u[rows, lane]), both_heads(query_v[rows, lane])
            relative = dot_right(place, offsets[start : start + SPAN, lane])
            scores = dot_right(content, key[:, lane])
            lows = []
            for head in range(2):
                part = slice(head * TILE, head * TILE + TILE)
                placed = pltpu.roll(relative[part], SPAN - TILE + 1, 1, stride=1, stride_axis=0)
                logits = scores[part] + placed[:, :LEN]
                expo = jnp.exp(logits - jnp.max(logits, axis=1, keepdims=True))
                lows.append(expo.astype(BF))
                probs[2 * pair + head, rows, :] = dot(mirror, lows[head]).astype(BF)
            outs = dot(jnp.concatenate(lows, axis=0), with_ones)
            outs = jnp.where(jnp.concatenate([head_mask(0, TILE)] * 2, axis=1), outs[:TILE], outs[TILE:])
            turned = 1.0 / outs[:, 128:]
            inverse[rows, lane] = turned
            mixed[rows, lane] = (outs[:, :128] * turned).astype(BF)
        return carry

    lax.fori_loop(0, 4, step, 0)


def depthwise(padded, vec, out, flip):
    def step(index, carry):
        lane = pl.multiple_of((index % 4) * 128, 128)
        first = pl.multiple_of((index // 4) * 64, 64)
        window = padded[pl.ds(first, 96), pl.ds(lane, 128)]
        total = None
        for shift in range(8):
            part = None
            for q in range(4):
                tap = 8 * q + shift - 1
                if tap < 0 or tap >= KERNEL:
                    continue
                tap = KERNEL - 1 - tap if flip else tap
                term = window[8 * q : 8 * q + 72] * vec[TAP + tap : TAP + tap + 1, pl.ds(lane, 128)]
                part = term if part is None else part + term
            part = part[shift : shift + 64]
            total = part if total is None else total + part
        out[pl.ds(first, 64), pl.ds(lane, 128)] = total
        return carry

    lax.fori_loop(0, 32, step, 0)


def fill(padded, values):
    padded[0:FRONT, :] = jnp.zeros((FRONT, WIDTH), F32)
    padded[FRONT : FRONT + LEN, :] = values
    padded[FRONT + LEN :, :] = jnp.zeros((PADDED - FRONT - LEN, WIDTH), F32)


def conv_front(mixed, x1, project, first, vec, x2, gates, gated, deep, stats, padded, wait, send):
    wait(5)
    after = x1[...] + dot(mixed[...], flat(project[...]))
    x2[...] = after
    normed, _ = normalise(after)
    conv_in = (normed * row(vec, GAIN + 2) + row(vec, SHIFT + 2)).astype(BF)
    wait(6)
    half = dot(conv_in, flat(first[:, 0:16, :]))
    gate = dot(conv_in, flat(first[:, 16:32, :]))
    gates[0] = half.astype(BF)
    gates[1] = gate.astype(BF)
    low = (half * sigmoid(gate)).astype(BF)
    gated[...] = low
    send(10, 11, 12)
    fill(padded, low.astype(F32))
    depthwise(padded, vec, deep, False)
    send(13)
    values = deep[...]
    spread(stats, (column_sum(values), column_sum(values * values)))


def begin(sources, targets, semaphores, ahead=()):
    copies = [
        pltpu.make_async_copy(source, target, semaphores.at[index])
        for index, (source, target) in enumerate(zip(sources, targets))
    ]
    for index in ahead:
        copies[index].start()
    for index, copy in enumerate(copies):
        if index not in ahead:
            copy.start()

    def wait(*which):
        for index in which:
            copies[index].wait()

    return wait


def front(
    bucket, frames, weights,
    x1_out, hidden_out, u_out, v_out, key_out, value_out, vec_out, probs_out, mixed_out, offsets_out,
    x2_out, gates_out, gated_out, deep_out, inverse_out, stats,
    x, small, matrix_in, matrix_out, project, table, last, first,
    x1, hidden, query_u, query_v, key, value, vec, probs, mixed, offsets, x2, gates, gated, deep,
    inverse, fed, broad, chosen, padded, arrived, left,
):
    wait = begin(
        [frames, weights.at[:, 384:400, 0:128]]
        + [weights.at[:, at : at + size, :] for at, size in ((128, 64), (256, 48), (368, 16), (304, 16), (320, 32))]
        + [weights.at[:, 16 * j : 16 + 16 * j, :] for j in range(4)],
        [x, small, matrix_out, project, table, last, first] + [matrix_in.at[:, :, chunk(j)] for j in range(4)],
        arrived,
        (0, 1, 7, 8, 9, 10),
    )
    held = [x1, hidden, query_u, query_v, key, value, vec, probs, mixed, offsets, x2, gates, gated, deep, inverse]
    outs = [
        x1_out, hidden_out, u_out, v_out, key_out, value_out, vec_out, probs_out, mixed_out, offsets_out,
        x2_out, gates_out, gated_out, deep_out, inverse_out,
    ]
    sent = [
        pltpu.make_async_copy(source, target, left.at[index])
        for index, (source, target) in enumerate(zip(held, outs))
    ]

    def send(*which):
        for index in which:
            sent[index].start()

    feed_front(x, small, matrix_in, matrix_out, project, x1, hidden, query_u, query_v, key, value, vec, fed, broad, wait)
    send(0, 1, 2, 3, 4, 5, 6)
    wait(4)
    attend(query_u, query_v, key, value, table, bucket, probs, mixed, offsets, inverse, chosen)
    send(7, 8, 9, 14)
    conv_front(mixed, x1, last, first, vec, x2, gates, gated, deep, stats, padded, wait, send)
    for copy in sent:
        copy.wait()


def batch_norm(stats, deep, vec):
    total, square = collect(stats)
    average = total / FRAMES
    inverse_root = lax.rsqrt(square / FRAMES - average * average + EPSILON)
    return (deep - average) * inverse_root, inverse_root


def feed_back(upstream, fed, hidden, matrix_in, matrix_out, kept, sent, u_low, broad, quarter, core):
    u_low[...] = upstream.astype(BF)
    side = lanes(u_low, quarter * 128, 128)
    for j in range(CHUNKS):
        part = hidden[j].astype(F32)
        logistic = sigmoid(part)
        active = (part * logistic).astype(BF)
        out_grad = dot_left(active, side)
        at = (slice(4 * j, 4 * j + 4), slice(64, 128))
        divide(core, kept, sent, at, out_grad.reshape(8, 64, 128))
        slope = logistic * (1.0 + part * (1.0 - logistic))
        back = dot_right(u_low[...], flat(matrix_out[8 * j : 8 * j + 8]))
        broad[:, chunk(j)] = (back * slope).astype(BF)
    pieces(core, kept, sent, 0, dot_left(fed[...], lanes(broad, quarter * 512, 512)))
    return dot_right(broad[...], flat(matrix_in[...]))


def centre(
    where, stats_in, deep_in, vec_in, x2_in, weights, cotangent_in,
    gx3_out, before_grad_out, y, stats_back, kept, sent, sums,
    deep, vec, x2, last, matrix_in, matrix_out, cotangent, gx3, before_grad,
    held_stats, fed, hidden, u_low, broad, wide, arrived, left,
):
    wait = begin(
        [deep_in, vec_in, weights.at[:, 352:368, :], x2_in, weights.at[:, 192:256, :], cotangent_in, stats_in]
        + [weights.at[:, 64 + 16 * j : 80 + 16 * j, :] for j in range(4)],
        [deep, vec, last, x2, matrix_out, cotangent, held_stats] + [matrix_in.at[:, :, chunk(j)] for j in range(4)],
        arrived,
        (6, 0, 1, 2, 3, 7, 8, 9, 10),
    )
    stats = held_stats
    wait(0, 1, 6)
    quarter, core = where[0], where[1]
    own = pl.ds(pl.multiple_of(quarter * TILE, TILE), TILE)
    centred, _ = batch_norm(stats, deep[...], vec)
    before = centred * row(vec, GAIN + 5) + row(vec, SHIFT + 5)
    swish = (before * sigmoid(before)).astype(BF)
    wait(2, 3)
    x3 = x2[...] + dot(swish, flat(last[...]))
    wide[...] = x3
    normed, inverse_root = normalise(x3)
    fed[...] = (normed * row(vec, GAIN + 3) + row(vec, SHIFT + 3)).astype(BF)
    wait(7, 8, 9, 10)
    forward_hidden(fed, matrix_in, hidden, broad)
    wait(4)
    x4 = wide[...] + 0.5 * dot(broad[...], flat(matrix_out[...]))
    normed4, inverse4 = normalise(x4)
    gx3[...] = normed4 * row(vec, GAIN + 4) + row(vec, SHIFT + 4)
    y[...] = gx3[own, :].astype(BF)
    wait(5)
    upstream = cotangent[...].astype(F32)
    sums[...] = jnp.zeros_like(sums)
    sums[2:3, :] = column_sum(upstream * normed4)
    sums[3:4, :] = column_sum(upstream)
    gx4 = norm_back(upstream, normed4, inverse4, row(vec, GAIN + 4))
    gx3[...] = gx4
    upstream = feed_back(0.5 * gx4, fed, hidden, matrix_in, matrix_out, kept, sent, u_low, broad, quarter, core)
    normed, inverse_root = normalise(wide[...])
    sums[0:1, :] = column_sum(upstream * normed)
    sums[1:2, :] = column_sum(upstream)
    after = gx3[...] + norm_back(upstream, normed, inverse_root, row(vec, GAIN + 3))
    gx3[...] = after
    gx3_sent = pltpu.make_async_copy(gx3, gx3_out, left.at[0])
    gx3_sent.start()
    u_low[...] = after.astype(BF)
    centred, _ = batch_norm(stats, deep[...], vec)
    before = centred * row(vec, GAIN + 5) + row(vec, SHIFT + 5)
    logistic = sigmoid(before)
    swish = (before * logistic).astype(BF)
    pieces(core, kept, sent, 128, dot_left(swish, lanes(u_low, quarter * 128, 128)))
    slope = logistic * (1.0 + before * (1.0 - logistic))
    back = dot_right(u_low[...], flat(last[...])) * slope
    before_grad[...] = back
    back_sent = pltpu.make_async_copy(before_grad, before_grad_out, left.at[1])
    back_sent.start()
    shift_sum, gain_sum = column_sum(back), column_sum(back * centred)
    sums[4:5, :] = gain_sum
    sums[5:6, :] = shift_sum
    spread(stats_back, (shift_sum, gain_sum))
    gx3_sent.wait()
    back_sent.wait()


def tap_grads(padded, padded_grad, acc):
    acc[...] = jnp.zeros_like(acc)

    def step(index, carry):
        lane = pl.multiple_of((index % 4) * 128, 128)
        first = pl.multiple_of((index // 4) * 104, 8)
        grad = padded_grad[pl.ds(first + 8, 112), pl.ds(lane, 128)]
        window = padded[pl.ds(first, 128), pl.ds(lane, 128)]
        for shift in range(8):
            moved = grad[8 - shift : 112 - shift]
            for q in range(4):
                tap = 8 * q + shift - 1
                if tap < 0 or tap >= KERNEL:
                    continue
                term = (window[8 * q : 8 * q + 104] * moved).reshape(13, 8, 128)
                acc[tap, :, pl.ds(lane, 128)] += jnp.sum(term, axis=0)
        return carry

    lax.fori_loop(0, 20, step, 0)


def conv_back(
    quarter, core, wait, before_grad, stats_back, stats, deep, gated, gates, x2, gx3, first, project, mixed, vec,
    gx2, mixed_grad, kept, sent, packed,
    padded, padded_grad, total, acc, both, u_low,
):
    wait(0, 1, 2, 26, 27)
    centred, inverse_root = batch_norm(stats, deep[...], vec)
    shift_sum, gain_sum = collect(stats_back)
    inner = before_grad[...] - shift_sum / FRAMES - centred * (gain_sum / FRAMES)
    low = (inverse_root * row(vec, GAIN + 5) * inner).astype(BF)
    fill(padded_grad, low.astype(F32))
    wait(3)
    fill(padded, gated[...].astype(F32))
    depthwise(padded_grad, vec, total, True)
    tap_grads(padded, padded_grad, acc)
    for tap in range(KERNEL):
        packed[TAP + tap : TAP + tap + 1, :] = column_sum(acc[tap])
    wait(4, 5, 6, 7, 8, 9)
    opened = sigmoid(gates[1].astype(F32))
    passed = total[...] * opened
    both[:, 0:WIDTH] = passed.astype(BF)
    both[:, WIDTH:] = (passed * gates[0].astype(F32) * (1.0 - opened)).astype(BF)
    normed, inverse_root = normalise(x2[...])
    conv_in = (normed * row(vec, GAIN + 2) + row(vec, SHIFT + 2)).astype(BF)
    pieces(core, kept, sent, 192, dot_left(conv_in, lanes(both, quarter * 256, 256)))
    upstream = dot_right(both[:, 0:WIDTH], flat(first[:, 0:16, :]))
    upstream = upstream + dot_right(both[:, WIDTH:], flat(first[:, 16:32, :]))
    packed[GAIN + 2 : GAIN + 3, :] = column_sum(upstream * normed)
    packed[SHIFT + 2 : SHIFT + 3, :] = column_sum(upstream)
    after = gx3[...] + norm_back(upstream, normed, inverse_root, row(vec, GAIN + 2))
    gx2[...] = after
    u_low[...] = after.astype(BF)
    pieces(core, kept, sent, 224, dot_left(mixed[...], lanes(u_low, quarter * 128, 128)))
    mixed_grad[...] = dot_right(u_low[...], flat(project[...])).astype(BF)


def attend_back(
    quarter, core, query_u, query_v, key, value, mixed_grad, probs, offsets, bucket, mixed, inverse,
    three, packed, kept, sent,
    score_grad, all_placed, turned, u_side, v_side, g_side, key_side, value_side, offset_grad,
):
    mirror = mirror_tile()
    left_tile = head_mask(0, TILE)

    def step(pair, carry):
        mine = quarter == pair

        def lane_at(base):
            return pl.ds(pl.multiple_of(base + pair * 128, 128), 128)

        lane = lane_at(0)
        for t in range(4):
            rows = slice(t * TILE, (t + 1) * TILE)
            upstream = (mixed_grad[rows, lane].astype(F32) * inverse[rows, lane]).astype(BF)
            turned[rows, :] = dot(mirror, upstream).astype(BF)
            u_side[:, rows] = dot_left(query_u[rows, lane], mirror).astype(BF)
            v_side[:, rows] = dot_left(query_v[rows, lane], mirror).astype(BF)
            g_side[:, rows] = dot_left(upstream, mirror).astype(BF)

        from_u, from_v = [], []
        for t in range(4):
            rows = slice(t * TILE, (t + 1) * TILE)
            start = LEN - TILE - TILE * t
            window = slice(start, start + SPAN)
            heads = both_heads(turned[rows, :])
            prob_grads = dot_right(heads, value[:, lane])
            mixed_rows = dot(mirror, mixed[rows, lane])
            lows, placed = [], []
            for head in range(2):
                part = slice(head * TILE, head * TILE + TILE)
                weighed = jnp.sum(heads[part].astype(F32) * mixed_rows, axis=1, keepdims=True)
                grad = probs[2 * pair + head, rows, :].astype(F32) * (prob_grads[part] - weighed)
                low = grad.astype(BF)
                score_grad[head, rows, :] = low
                lows.append(low)
                padded = jnp.concatenate([grad, jnp.zeros((TILE, TILE), F32)], axis=1)
                placed.append(pltpu.roll(padded, 0, 1, stride=1, stride_axis=0).astype(BF))
                all_placed[head, rows, :] = placed[head]
            u_parts = dot(jnp.concatenate(lows, axis=0), key[:, lane])
            v_parts = dot(jnp.concatenate(placed, axis=0), offsets[window, lane])

            u_part = jnp.where(left_tile, u_parts[:TILE], u_parts[TILE:]) * 0.125
            v_part = jnp.where(left_tile, v_parts[:TILE], v_parts[TILE:]) * 0.125
            from_u.append(column_sum(u_part))
            from_v.append(column_sum(v_part))
            three[rows, lane] = dot(mirror, (u_part + v_part).astype(BF)).astype(BF)
        for head in range(2):
            side = slice(64 * head, 64 * head + 64)
            key_side[side, :] = dot(u_side[side, :], score_grad[head])
            value_side[side, :] = dot(g_side[side, :], probs[2 * pair + head])
        three[:, lane_at(WIDTH)] = key_side[...].T.astype(BF)
        three[:, lane_at(2 * WIDTH)] = value_side[...].T.astype(BF)
        packed[SHIFT + 6 : SHIFT + 7, lane] = from_u[0] + from_u[1] + from_u[2] + from_u[3]
        packed[SHIFT + 7 : SHIFT + 8, lane] = from_v[0] + from_v[1] + from_v[2] + from_v[3]

        @pl.when(mine)
        def _():
            offset_grad[...] = jnp.zeros_like(offset_grad)
            for t in range(4):
                rows = slice(t * TILE, (t + 1) * TILE)
                window = slice(LEN - TILE - TILE * t, 2 * LEN - TILE * t)
                for head in range(2):
                    side = slice(64 * head, 64 * head + 64)
                    offset_grad[side, window] += dot(v_side[side, rows], all_placed[head, rows, :])
            number = lax.broadcasted_iota(jnp.int32, (2 * LEN, 256), 1)
            chosen = (bucket[...] == number).astype(F32).astype(BF)
            table_grad = dot(offset_grad[...].astype(BF), chosen).T.reshape(32, 8, 128)
            table_grad = jnp.concatenate([table_grad, jnp.zeros((32, 8, 128), F32)], axis=1)
            divide(core, kept, sent, (slice(None), slice(240, 256)), table_grad)

        return carry

    lax.fori_loop(0, 4, step, 0)


def feed_last(
    quarter, core, wait, x1, gx2, project, matrix_in, matrix_out, hidden, x, vec, sums4,
    gx0, kept, sent,
    three, fed, u_low, broad, wide, packed,
):
    own = pl.ds(pl.multiple_of(quarter * TILE, TILE), TILE)
    wait(16, 17, 18, 19, 20, 21, 22, 23, 24)
    normed, inverse_root = normalise(x1[...])
    attn_in = (normed * row(vec, GAIN + 1) + row(vec, SHIFT + 1)).astype(BF)
    pieces(core, kept, sent, 128, dot_left(attn_in, lanes(three, quarter * 384, 384)))
    upstream = dot_right(three[:, 0:WIDTH], flat(project[:, 0:16, :]))
    upstream = upstream + dot_right(three[:, WIDTH : 2 * WIDTH], flat(project[:, 16:32, :]))
    upstream = upstream + dot_right(three[:, 2 * WIDTH :], flat(project[:, 32:48, :]))
    packed[GAIN + 1 : GAIN + 2, :] = column_sum(upstream * normed)
    packed[SHIFT + 1 : SHIFT + 2, :] = column_sum(upstream)
    gx1 = gx2[...] + norm_back(upstream, normed, inverse_root, row(vec, GAIN + 1))
    wide[...] = gx1
    normed, inverse_root = normalise(x[...].astype(F32))
    fed[...] = (normed * row(vec, GAIN) + row(vec, SHIFT)).astype(BF)
    upstream = feed_back(0.5 * gx1, fed, hidden, matrix_in, matrix_out, kept, sent, u_low, broad, quarter, core)
    normed, inverse_root = normalise(x[...].astype(F32))
    packed[GAIN : GAIN + 1, :] = column_sum(upstream * normed)
    packed[SHIFT : SHIFT + 1, :] = column_sum(upstream)
    wide[...] = wide[...] + norm_back(upstream, normed, inverse_root, row(vec, GAIN))
    gx0[...] = wide[own, :]
    for index in range(3):
        packed[GAIN + 3 + index : GAIN + 4 + index, :] = row(sums4, 2 * index)
        packed[SHIFT + 3 + index : SHIFT + 4 + index, :] = row(sums4, 2 * index + 1)
    pieces(core, kept, sent, 176, packed[...].T)


def back(
    where, bucket, sums4, stats_back_in, stats_in,
    before_in, deep_in, vec_in, gated_in, gates_in, x2_in, weights, gx3_in, mixed_in,
    u_in, v_in, key_in, value_in, probs_in, offsets_in, x1_in, hidden_in, frames, inverse_in,
    gx0, kept, sent,
    before_grad, deep, vec, gated, gates, x2, first, gx3, last, mixed,
    query_u, query_v, key, value, probs, offsets, x1, project, matrix_in, matrix_out, hidden, x,
    inverse, stats_back, stats, gx2, mixed_grad, packed, padded, padded_grad, total, acc, both, u_low,
    three, score_grad, all_placed, turned, u_side, v_side, g_side, key_side, value_side, offset_grad,
    fed, broad, wide, arrived,
):
    quarter, core = where[0], where[1]

    def part(at, size):
        return weights.at[:, at : at + size, :]

    wait = begin(
        [before_in, deep_in, vec_in, gated_in, gates_in, x2_in, part(320, 32), gx3_in, part(304, 16), mixed_in]
        + [value_in, probs_in, key_in, offsets_in, u_in, v_in]
        + [x1_in, part(256, 48), part(128, 64), hidden_in, frames]
        + [part(16 * j, 16) for j in range(4)]
        + [inverse_in, stats_back_in, stats_in],
        [before_grad, deep, vec, gated, gates, x2, first, gx3, last, mixed]
        + [value, probs, key, offsets, query_u, query_v]
        + [x1, project, matrix_out, hidden, x]
        + [matrix_in.at[:, :, chunk(j)] for j in range(4)]
        + [inverse, stats_back, stats],
        arrived,
        (26, 27),
    )
    packed[...] = jnp.zeros_like(packed)
    conv_back(
        quarter, core, wait, before_grad, stats_back, stats, deep, gated, gates, x2, gx3, first, last, mixed, vec,
        gx2, mixed_grad, kept, sent, packed,
        padded, padded_grad, total, acc, both, u_low,
    )
    wait(10, 11, 12, 13, 14, 15, 25)
    attend_back(
        quarter, core, query_u, query_v, key, value, mixed_grad, probs, offsets, bucket, mixed, inverse,
        three, packed, kept, sent,
        score_grad, all_placed, turned, u_side, v_side, g_side, key_side, value_side, offset_grad,
    )
    feed_last(
        quarter, core, wait, x1, gx2, project, matrix_in, matrix_out, hidden, x, vec, sums4,
        gx0, kept, sent,
        three, fed, u_low, broad, wide, packed,
    )


def unpack(
    where, part0, part1, part2, part3,
    g_in, g_out, g_project, g_last, g_table, g_first, g_taps, g_conv, g_gain, g_shift,
):
    for hop, part in enumerate((part0, part1, part2, part3)):
        side = lax.rem(where[0] + 4 - hop, 4)

        def put(out, first, rows, wide, lane, m=None, part=part, side=side):
            at = pl.ds(pl.multiple_of(side * wide + lane * 128, 128), 128)
            block = part[first : first + rows, :].astype(F32)
            if m is None:
                out[:, at] = block[0 : out.shape[0]]
            else:
                out[m, :, at] = block

        for m, base in ((0, 0), (1, 256)):
            for lane in range(4):
                put(g_in, base + 16 * lane, 16, 512, lane, m)
            put(g_out, base + 64, 64, 128, 0, m)
        for lane in range(3):
            put(g_project, 128 + 16 * lane, 16, 384, lane)
        for lane in range(2):
            put(g_first, 192 + 16 * lane, 16, 256, lane)
        put(g_last, 224, 16, 128, 0)
        put(g_conv, 384, 16, 128, 0)
        put(g_table, 240, 16, 128, 0)
    vectors = part0[176:192, :].astype(F32)
    g_taps[...] = vectors[:, TAP : TAP + KERNEL]
    vectors = vectors.T
    for index in range(6):
        g_gain[index] = row(vectors, GAIN + index)
    g_shift[...] = vectors[SHIFT : SHIFT + 8]


def whole(shape):
    return pl.BlockSpec(shape, lambda *at: (0,) * len(shape), pipeline_mode=pl.Buffered(1))


WHERE = pl.BlockSpec(memory_space=pltpu.SMEM)
FULL = (LEN, WIDTH)
LIMIT = 56 << 20


ANYWHERE = pl.BlockSpec(memory_space=pl.ANY)


def call(kernel, micros, in_specs, outs, scratch, far=0, semaphores=()):
    return pl.pallas_call(
        kernel,
        grid=(1,),
        in_specs=in_specs,
        out_specs=[ANYWHERE if at < far else whole(shape) for at, (shape, _) in enumerate(outs)],
        out_shape=[jax.ShapeDtypeStruct(shape, dtype) for shape, dtype in outs],
        scratch_shapes=[pltpu.VMEM(shape, dtype) for shape, dtype in scratch]
        + [pltpu.SemaphoreType.DMA((count,)) for count in semaphores],
        compiler_params=pltpu.CompilerParams(vmem_limit_bytes=LIMIT),
        cost_estimate=pl.CostEstimate(flops=micros * 1150 * 10**6, bytes_accessed=0, transcendentals=0),
    )


def share(stats):
    return lax.all_to_all(stats, ("y", "z", "c"), 0, 0, tiled=True)


def with_core(kept, sent):
    other = lax.ppermute(sent, "c", [(0, 1), (1, 0)])
    return (kept.astype(F32) + other.astype(F32)).astype(BF)


def across(chip):
    return lax.all_to_all(chip, ("y", "z"), 0, 0, tiled=True)


def total_of(chip):
    return jnp.sum(chip.astype(F32), axis=0).astype(BF)


def shards(
    inputs, matrices_in, matrices_out, project_in, project_out, pos_table, conv_first, depth_taps,
    conv_last, gain_rows, shift_rows, bucket, cotangent,
):
    fsdp = ("y", "z", "c")
    where = jnp.stack([lax.axis_index("x"), lax.axis_index("c")]).astype(jnp.int32)

    packed = call(
        pack,
        2,
        [whole(part.shape) for part in (matrices_in, matrices_out, project_in, project_out, pos_table, conv_first)]
        + [whole((16, KERNEL)), whole(conv_last.shape), whole(gain_rows.shape), whole(shift_rows.shape)],
        [((400, WIDTH), BF)],
        [((128, 16), F32)],
    )(
        matrices_in, matrices_out, project_in, project_out, pos_table, conv_first,
        jnp.transpose(depth_taps, (0, 2, 1))[0], conv_last, gain_rows, shift_rows,
    )[0]
    weights = lax.all_gather(packed, fsdp, axis=0, tiled=False)
    frames = lax.all_gather(inputs[0], "x", axis=0, tiled=True)
    upstream = lax.all_gather(cotangent[0], "x", axis=0, tiled=True)
    frames, upstream = lax.optimization_barrier((frames, upstream))
    reversed_bucket = jnp.concatenate([bucket[::-1], jnp.full((1,), -1, jnp.int32)])
    tall = reversed_bucket.reshape(2 * LEN, 1)

    full, low, stats_shape = (FULL, F32), (FULL, BF), ((32, 8, 128), F32)
    vec_shape, four = ((128, WIDTH), F32), ((4,) + FULL, BF)
    two, probs_shape, offsets_shape = ((2,) + FULL, BF), ((8, LEN, LEN), BF), ((2 * LEN, WIDTH), BF)
    tall_spec = whole((2 * LEN, 1))

    def rows_of(size):
        return ((32, size, WIDTH), BF)

    held = [full, four, low, low, low, low, vec_shape, probs_shape, low, offsets_shape, full, two, low, full, full]
    broad = ((LEN, 2048), BF)
    wide_in = ((32, 16, 2048), BF)
    (
        x1, hidden, query_u, query_v, key, value, vec, probs, mixed, offsets, x2, gates, gated, deep, inverse, stats,
    ) = call(
        front,
        28,
        [tall_spec, ANYWHERE, ANYWHERE],
        held + [stats_shape],
        [low, ((32, 16, 128), BF), wide_in, rows_of(64), rows_of(48), rows_of(16), rows_of(16), rows_of(32)]
        + held
        + [low, broad, ((2 * LEN, 256), BF), ((PADDED, WIDTH), F32)],
        far=15,
        semaphores=(11, 15),
    )(tall, frames, weights)
    stats = share(stats)

    gx3, before_grad, y, stats_back, kept4, sent4, sums4 = call(
        centre,
        12,
        [WHERE] + [ANYWHERE] * 6,
        [full, full, ((TILE, WIDTH), BF), stats_shape, ((16, 144, 128), BF), ((16, 144, 128), BF), ((8, WIDTH), F32)],
        [full, vec_shape, full, rows_of(16), wide_in, rows_of(64), low, full, full]
        + [stats_shape, low, four, low, broad, full],
        far=2,
        semaphores=(11, 2),
    )(where, stats, deep, vec, x2, weights, upstream)
    stats_back = share(stats_back)

    gx0, kept, sent = call(
        back,
        42,
        [WHERE, tall_spec, whole((8, WIDTH))] + [ANYWHERE] * 21,
        [((TILE, WIDTH), F32), ((16, 256, 128), BF), ((16, 256, 128), BF)],
        [full, full, vec_shape, low, two, full, rows_of(32), full, rows_of(16), low]
        + [low, low, low, low, probs_shape, offsets_shape, full, rows_of(48), wide_in, rows_of(64), four, low]
        + [full, stats_shape, stats_shape]
        + [full, low, vec_shape, ((PADDED, WIDTH), F32), ((PADDED, WIDTH), F32), full, ((KERNEL, 8, WIDTH), F32)]
        + [((LEN, 2 * WIDTH), BF), low, ((LEN, 3 * WIDTH), BF), two, ((2, LEN, SPAN), BF), ((LEN, 128), BF)]
        + [((128, LEN), BF)] * 3 + [((128, LEN), F32)] * 2 + [((128, 2 * LEN), F32)]
        + [low, broad, full],
        semaphores=(28,),
    )(
        where, tall, sums4, stats_back, stats,
        before_grad, deep, vec, gated, gates, x2, weights, gx3, mixed,
        query_u, query_v, key, value, probs, offsets, x1, hidden, frames, inverse,
    )
    chips = [with_core(kept, sent), with_core(kept4, sent4)]
    total = total_of(across(jnp.concatenate(chips, axis=1)))
    hops = [[(i, (i + hop) % 4) for i in range(4)] for hop in range(4)]
    parts = [total] + [lax.ppermute(total, "x", hops[hop]) for hop in (1, 2, 3)]
    results = call(
        unpack,
        2,
        [WHERE] + [whole(total.shape)] * 4,
        [((2, 16, 2048), F32), ((2, 64, 512), F32), ((16, 1536), F32), ((16, 512), F32), ((8, 512), F32),
         ((16, 1024), F32), ((16, KERNEL), F32), ((16, 512), F32), ((6, 1, 16), F32), ((8, 16), F32)],
        [],
    )(where, *parts)
    results = list(results)
    results[6] = results[6].T
    results[8] = results[8][:, 0]
    return (y[None], gx0[None]) + tuple(result[None] for result in results)


def solution(mesh):
    fine = Mesh(mesh.devices.reshape(4, 4, 2, 4), ("y", "z", "c", "x"))
    fsdp = ("y", "z", "c")
    activations = P(fsdp, "x", None)
    placed = (
        activations,
        P(None, None, fsdp, None),
        P(None, None, fsdp, None),
        P(None, fsdp, None),
        P(None, fsdp, None),
        P(None, fsdp, None),
        P(None, fsdp, None),
        P(None, None, fsdp),
        P(None, fsdp, None),
        P(None, None, fsdp),
        P(None, None, fsdp),
    )
    return jax.shard_map(
        shards,
        mesh=fine,
        in_specs=placed + (P(), activations),
        out_specs=(activations, activations) + placed[1:],
        check_vma=False,
    )
```

```python
import functools

import jax
import jax.numpy as jnp
from jax import lax
from jax.experimental import pallas as pl
from jax.experimental.pallas import tpu as pltpu
from jax.sharding import Mesh
from jax.sharding import PartitionSpec as P

EPSILON = 1e-05
KERNEL = 31
LEN = 512
WIDTH = 512
CHUNKS = 4
TILE = 128
SPAN = TILE + LEN
FRAMES = 16384
BF = jnp.bfloat16
F32 = jnp.float32
GAIN, SHIFT, TAP = 0, 6, 14
FRONT = 16
PADDED = 560


def dot(left, right):
    return lax.dot_general(left, right, (((1,), (0,)), ((), ())), preferred_element_type=F32)


def dot_right(left, right):
    return lax.dot_general(left, right, (((1,), (1,)), ((), ())), preferred_element_type=F32)


def dot_left(left, right):
    return lax.dot_general(left, right, (((0,), (0,)), ((), ())), preferred_element_type=F32)


def normalise(values):
    centred = values - jnp.mean(values, axis=-1, keepdims=True)
    inverse_root = lax.rsqrt(jnp.mean(centred * centred, axis=-1, keepdims=True) + EPSILON)
    return centred * inverse_root, inverse_root


def norm_back(upstream, normed, inverse_root, gain):
    scaled = upstream * gain
    inner = (
        scaled
        - jnp.mean(scaled, axis=-1, keepdims=True)
        - normed * jnp.mean(scaled * normed, axis=-1, keepdims=True)
    )
    return inverse_root * inner


def sigmoid(values):
    return 0.5 * jnp.tanh(0.5 * values) + 0.5


def column_sum(values):
    return jnp.sum(values, axis=0, keepdims=True)


def row(vec, index):
    return vec[index : index + 1, :]


def flat(block):
    return block.reshape(block.shape[0] * block.shape[1], block.shape[2])


def divide(core, kept, sent, at, block):
    block = block.reshape(block.shape[0] // 2, 2, block.shape[1], 128).astype(BF)
    first, second = block[:, 0], block[:, 1]
    kept[at] = jnp.where(core == 0, first, second)
    sent[at] = jnp.where(core == 0, second, first)


def pieces(core, kept, sent, first, grad):
    for lane in range(grad.shape[1] // 128):
        part = grad[:, lane * 128 : (lane + 1) * 128]
        high = part.shape[0] // 32
        at = (slice(None), slice(first + lane * high, first + lane * high + high))
        divide(core, kept, sent, at, part.reshape(32, high, 128))


def lanes(ref, start, size):
    return ref[:, pl.ds(pl.multiple_of(start, 128), size)]


def spread(out, sums):
    for which in range(2):
        for lane in range(4):
            line = sums[which][:, lane * 128 : (lane + 1) * 128]
            out[:, 4 * which + lane, :] = jnp.broadcast_to(line, (32, 128))


def collect(stats):
    total = jnp.sum(stats[...], axis=0)
    return [
        jnp.concatenate([total[4 * which + lane : 4 * which + lane + 1] for lane in range(4)], axis=1)
        for which in range(2)
    ]


def pack(m_in, m_out, project, last, table, first, taps, conv, gain, shift, out, small):
    for m in range(2):
        for j in range(4):
            at = 64 * m + 16 * j
            out[at : at + 16, :] = m_in[0, m, :, 512 * j : 512 * j + 512]
        out[128 + 64 * m : 192 + 64 * m, :] = m_out[0, m]
    for j in range(3):
        out[256 + 16 * j : 272 + 16 * j, :] = project[0, :, 512 * j : 512 * j + 512]
    out[304:320, :] = last[0]
    for j in range(2):
        out[320 + 16 * j : 336 + 16 * j, :] = first[0, :, 512 * j : 512 * j + 512]
    out[352:368, :] = conv[0]
    table_rows = table[0].astype(F32)
    out[368:384, :] = jnp.concatenate([table_rows, jnp.zeros_like(table_rows)], axis=0).astype(BF)
    small[...] = jnp.zeros_like(small)
    small[GAIN : GAIN + 6, :] = gain[0].astype(F32)
    small[SHIFT : SHIFT + 8, :] = shift[0].astype(F32)
    small[TAP : TAP + KERNEL, :] = taps[...].astype(F32).T
    out[384:400, :] = jnp.zeros((16, WIDTH), BF)
    out[384:400, 0:128] = small[...].T.astype(BF)


def chunk(j):
    return slice(512 * j, 512 * j + 512)


def forward_hidden(fed, matrix_in, hidden, broad):
    for j in range(CHUNKS):
        part = dot(fed[...], flat(matrix_in[:, :, chunk(j)]))
        hidden[j] = part.astype(BF)
        broad[:, chunk(j)] = (part * sigmoid(part)).astype(BF)


def feed_front(x, small, matrix_in, matrix_out, project, x1, hidden, query_u, query_v, key, value, vec, fed, broad, start, wait):
    wait(0, 1)
    start(1)
    vec[...] = flat(small[...]).astype(F32).T
    values = x[...].astype(F32)
    normed, _ = normalise(values)
    fed[...] = (normed * row(vec, GAIN) + row(vec, SHIFT)).astype(BF)
    wait(7, 8, 9, 10)
    start(2)
    forward_hidden(fed, matrix_in, hidden, broad)
    wait(2)
    after = values + 0.5 * dot(broad[...], flat(matrix_out[...]))
    x1[...] = after
    normed, _ = normalise(after)
    fed[...] = (normed * row(vec, GAIN + 1) + row(vec, SHIFT + 1)).astype(BF)
    wait(3)
    query = dot(fed[...], flat(project[:, 0:16, :]))
    query_u[...] = ((query + row(vec, SHIFT + 6)) * 0.125).astype(BF)
    query_v[...] = ((query + row(vec, SHIFT + 7)) * 0.125).astype(BF)
    key[...] = dot(fed[...], flat(project[:, 16:32, :])).astype(BF)
    value[...] = dot(fed[...], flat(project[:, 32:48, :])).astype(BF)


def head_mask(which, rows):
    lane = lax.broadcasted_iota(jnp.int32, (rows, 128), 1)
    return (lane < 64) if which == 0 else (lane >= 64)


def mirror_tile():
    row_at = lax.broadcasted_iota(jnp.int32, (TILE, TILE), 0)
    column_at = lax.broadcasted_iota(jnp.int32, (TILE, TILE), 1)
    return (row_at + column_at == TILE - 1).astype(F32).astype(BF)


def triangle():
    row_at = lax.broadcasted_iota(jnp.int32, (TILE, TILE), 0)
    return lax.broadcasted_iota(jnp.int32, (TILE, TILE), 1) - row_at


def skew(block, below):
    turns = [
        pltpu.roll(block[:, 128 * k : 128 * k + 128], 1, 1, stride=1, stride_axis=0) for k in range(5)
    ]
    return jnp.concatenate([jnp.where(below, turns[k], turns[k + 1]) for k in range(4)], axis=1)


def unskew(block, above):
    turns = [
        pltpu.roll(block[:, 128 * k : 128 * k + 128], 0, 1, stride=1, stride_axis=0) for k in range(4)
    ]
    parts = [jnp.where(above, turns[0], 0.0)]
    parts += [jnp.where(above, turns[k], turns[k - 1]) for k in range(1, 4)]
    return jnp.concatenate(parts + [jnp.where(above, 0.0, turns[3])], axis=1)


def both_heads(block):
    halves = [jnp.where(head_mask(head, TILE), block, 0.0).astype(BF) for head in range(2)]
    return jnp.concatenate(halves, axis=0)


def attend(query_u, query_v, key, value, table, bucket, probs, mixed, offsets, inverse, chosen):
    number = lax.broadcasted_iota(jnp.int32, (2 * LEN, 256), 1)
    chosen[...] = (bucket[...] == number).astype(F32).astype(BF)
    mirror = mirror_tile()
    below = triangle() <= 0

    def step(pair, carry):
        lane = pl.ds(pl.multiple_of(pair * 128, 128), 128)
        table_rows = table[:, :, lane].astype(F32)[:, 0:8, :].reshape(256, 128).astype(BF)
        offsets[:, lane] = dot(chosen[...], table_rows).astype(BF)
        with_ones = jnp.concatenate([value[:, lane], jnp.ones((LEN, 128), BF)], axis=1)
        for t in range(4):
            rows = slice(t * TILE, (t + 1) * TILE)
            start = LEN - TILE - TILE * t
            content, place = both_heads(query_u[rows, lane]), both_heads(query_v[rows, lane])
            relative = dot_right(place, offsets[start : start + SPAN, lane])
            scores = dot_right(content, key[:, lane])
            lows = []
            for head in range(2):
                part = slice(head * TILE, head * TILE + TILE)
                logits = scores[part] + skew(relative[part], below)
                expo = jnp.exp(logits - jnp.max(logits, axis=1, keepdims=True))
                lows.append(expo.astype(BF))
                probs[2 * pair + head, rows, :] = dot(mirror, lows[head]).astype(BF)
            outs = dot(jnp.concatenate(lows, axis=0), with_ones)
            outs = jnp.where(jnp.concatenate([head_mask(0, TILE)] * 2, axis=1), outs[:TILE], outs[TILE:])
            turned = 1.0 / outs[:, 128:]
            inverse[rows, lane] = turned
            mixed[rows, lane] = (outs[:, :128] * turned).astype(BF)
        return carry

    lax.fori_loop(0, 4, step, 0, unroll=2)


def depthwise(padded, vec, out, flip):
    def step(index, carry):
        lane = pl.multiple_of((index % 4) * 128, 128)
        first = pl.multiple_of((index // 4) * 64, 64)
        window = padded[pl.ds(first, 96), pl.ds(lane, 128)]
        total = None
        for shift in range(8):
            part = None
            for q in range(4):
                tap = 8 * q + shift - 1
                if tap < 0 or tap >= KERNEL:
                    continue
                tap = KERNEL - 1 - tap if flip else tap
                term = window[8 * q : 8 * q + 72] * vec[TAP + tap : TAP + tap + 1, pl.ds(lane, 128)]
                part = term if part is None else part + term
            part = part[shift : shift + 64]
            total = part if total is None else total + part
        out[pl.ds(first, 64), pl.ds(lane, 128)] = total
        return carry

    lax.fori_loop(0, 32, step, 0)


def fill(padded, values):
    padded[0:FRONT, :] = jnp.zeros((FRONT, WIDTH), F32)
    padded[FRONT : FRONT + LEN, :] = values
    padded[FRONT + LEN :, :] = jnp.zeros((PADDED - FRONT - LEN, WIDTH), F32)


def conv_front(mixed, x1, project, first, vec, x2, gates, gated, deep, stats, padded, wait, send):
    wait(5)
    after = x1[...] + dot(mixed[...], flat(project[...]))
    x2[...] = after
    normed, _ = normalise(after)
    conv_in = (normed * row(vec, GAIN + 2) + row(vec, SHIFT + 2)).astype(BF)
    wait(6)
    half = dot(conv_in, flat(first[:, 0:16, :]))
    gate = dot(conv_in, flat(first[:, 16:32, :]))
    gates[0] = half.astype(BF)
    gates[1] = gate.astype(BF)
    low = (half * sigmoid(gate)).astype(BF)
    gated[...] = low
    send(10, 11, 12)
    fill(padded, low.astype(F32))
    depthwise(padded, vec, deep, False)
    send(13)
    values = deep[...]
    spread(stats, (column_sum(values), column_sum(values * values)))


def begin(sources, targets, semaphores, *groups):
    copies = [
        pltpu.make_async_copy(source, target, semaphores.at[index])
        for index, (source, target) in enumerate(zip(sources, targets))
    ]

    def start(group):
        for index in groups[group]:
            copies[index].start()

    def wait(*which):
        for index in which:
            copies[index].wait()

    start(0)
    return start, wait


def front(
    frames, weights, bucket_in,
    x1_out, hidden_out, u_out, v_out, key_out, value_out, vec_out, probs_out, mixed_out, offsets_out,
    x2_out, gates_out, gated_out, deep_out, inverse_out, stats,
    x, small, matrix_in, matrix_out, project, table, last, first, bucket,
    x1, hidden, query_u, query_v, key, value, vec, probs, mixed, offsets, x2, gates, gated, deep,
    inverse, fed, broad, chosen, padded, arrived, left,
):
    start, wait = begin(
        [frames, weights.at[:, 384:400, 0:128]]
        + [weights.at[:, at : at + size, :] for at, size in ((128, 64), (256, 48), (368, 16), (304, 16), (320, 32))]
        + [weights.at[:, 16 * j : 16 + 16 * j, :] for j in range(4)]
        + [bucket_in],
        [x, small, matrix_out, project, table, last, first] + [matrix_in.at[:, :, chunk(j)] for j in range(4)] + [bucket],
        arrived,
        (0, 1, 7, 8, 9, 10),
        (2, 3),
        (4, 11, 5, 6),
    )
    held = [x1, hidden, query_u, query_v, key, value, vec, probs, mixed, offsets, x2, gates, gated, deep, inverse]
    outs = [
        x1_out, hidden_out, u_out, v_out, key_out, value_out, vec_out, probs_out, mixed_out, offsets_out,
        x2_out, gates_out, gated_out, deep_out, inverse_out,
    ]
    sent = [
        pltpu.make_async_copy(source, target, left.at[index])
        for index, (source, target) in enumerate(zip(held, outs))
    ]

    def send(*which):
        for index in which:
            sent[index].start()

    feed_front(x, small, matrix_in, matrix_out, project, x1, hidden, query_u, query_v, key, value, vec, fed, broad, start, wait)
    send(0, 1, 2, 3, 4, 5, 6)
    wait(4, 11)
    attend(query_u, query_v, key, value, table, bucket, probs, mixed, offsets, inverse, chosen)
    send(7, 8, 9, 14)
    conv_front(mixed, x1, last, first, vec, x2, gates, gated, deep, stats, padded, wait, send)
    for copy in sent:
        copy.wait()


def batch_norm(stats, deep, vec):
    total, square = collect(stats)
    average = total / FRAMES
    inverse_root = lax.rsqrt(square / FRAMES - average * average + EPSILON)
    return (deep - average) * inverse_root, inverse_root


def feed_back(upstream, fed, hidden, matrix_in, matrix_out, kept, sent, u_low, broad, quarter, core):
    u_low[...] = upstream.astype(BF)
    side = lanes(u_low, quarter * 128, 128)
    for j in range(CHUNKS):
        part = hidden[j].astype(F32)
        logistic = sigmoid(part)
        active = (part * logistic).astype(BF)
        out_grad = dot_left(active, side)
        at = (slice(4 * j, 4 * j + 4), slice(64, 128))
        divide(core, kept, sent, at, out_grad.reshape(8, 64, 128))
        slope = logistic * (1.0 + part * (1.0 - logistic))
        back = dot_right(u_low[...], flat(matrix_out[8 * j : 8 * j + 8]))
        broad[:, chunk(j)] = (back * slope).astype(BF)
    pieces(core, kept, sent, 0, dot_left(fed[...], lanes(broad, quarter * 512, 512)))
    return dot_right(broad[...], flat(matrix_in[...]))


def centre(
    where, stats_in, deep_in, vec_in, x2_in, weights, cotangent_in,
    gx3_out, before_grad_out, y, stats_back, kept, sent, sums,
    deep, vec, x2, last, matrix_in, matrix_out, cotangent, gx3, before_grad,
    held_stats, fed, hidden, u_low, broad, wide, arrived, left,
):
    start, wait = begin(
        [deep_in, vec_in, weights.at[:, 352:368, :], x2_in, weights.at[:, 192:256, :], cotangent_in, stats_in]
        + [weights.at[:, 64 + 16 * j : 80 + 16 * j, :] for j in range(4)],
        [deep, vec, last, x2, matrix_out, cotangent, held_stats] + [matrix_in.at[:, :, chunk(j)] for j in range(4)],
        arrived,
        (6, 0, 1, 2, 3, 7, 8, 9, 10, 4, 5),
    )
    stats = held_stats
    wait(0, 1, 6)
    quarter, core = where[0], where[1]
    own = pl.ds(pl.multiple_of(quarter * TILE, TILE), TILE)
    centred, _ = batch_norm(stats, deep[...], vec)
    before = centred * row(vec, GAIN + 5) + row(vec, SHIFT + 5)
    swish = (before * sigmoid(before)).astype(BF)
    wait(2, 3)
    x3 = x2[...] + dot(swish, flat(last[...]))
    wide[...] = x3
    normed, inverse_root = normalise(x3)
    fed[...] = (normed * row(vec, GAIN + 3) + row(vec, SHIFT + 3)).astype(BF)
    wait(7, 8, 9, 10)
    forward_hidden(fed, matrix_in, hidden, broad)
    wait(4)
    x4 = wide[...] + 0.5 * dot(broad[...], flat(matrix_out[...]))
    normed4, inverse4 = normalise(x4)
    gx3[...] = normed4 * row(vec, GAIN + 4) + row(vec, SHIFT + 4)
    y[...] = gx3[own, :].astype(BF)
    wait(5)
    upstream = cotangent[...].astype(F32)
    sums[...] = jnp.zeros_like(sums)
    sums[2:3, :] = column_sum(upstream * normed4)
    sums[3:4, :] = column_sum(upstream)
    gx4 = norm_back(upstream, normed4, inverse4, row(vec, GAIN + 4))
    gx3[...] = gx4
    upstream = feed_back(0.5 * gx4, fed, hidden, matrix_in, matrix_out, kept, sent, u_low, broad, quarter, core)
    normed, inverse_root = normalise(wide[...])
    sums[0:1, :] = column_sum(upstream * normed)
    sums[1:2, :] = column_sum(upstream)
    after = gx3[...] + norm_back(upstream, normed, inverse_root, row(vec, GAIN + 3))
    gx3[...] = after
    gx3_sent = pltpu.make_async_copy(gx3, gx3_out, left.at[0])
    gx3_sent.start()
    u_low[...] = after.astype(BF)
    centred, _ = batch_norm(stats, deep[...], vec)
    before = centred * row(vec, GAIN + 5) + row(vec, SHIFT + 5)
    logistic = sigmoid(before)
    swish = (before * logistic).astype(BF)
    pieces(core, kept, sent, 128, dot_left(swish, lanes(u_low, quarter * 128, 128)))
    slope = logistic * (1.0 + before * (1.0 - logistic))
    back = dot_right(u_low[...], flat(last[...])) * slope
    before_grad[...] = back
    back_sent = pltpu.make_async_copy(before_grad, before_grad_out, left.at[1])
    back_sent.start()
    shift_sum, gain_sum = column_sum(back), column_sum(back * centred)
    sums[4:5, :] = gain_sum
    sums[5:6, :] = shift_sum
    spread(stats_back, (shift_sum, gain_sum))
    gx3_sent.wait()
    back_sent.wait()


def tap_grads(padded, padded_grad, acc):
    acc[...] = jnp.zeros_like(acc)

    def step(index, carry):
        lane = pl.multiple_of((index % 4) * 128, 128)
        first = pl.multiple_of((index // 4) * 104, 8)
        grad = padded_grad[pl.ds(first + 8, 112), pl.ds(lane, 128)]
        window = padded[pl.ds(first, 128), pl.ds(lane, 128)]
        for shift in range(8):
            moved = grad[8 - shift : 112 - shift]
            for q in range(4):
                tap = 8 * q + shift - 1
                if tap < 0 or tap >= KERNEL:
                    continue
                term = (window[8 * q : 8 * q + 104] * moved).reshape(13, 8, 128)
                acc[tap, :, pl.ds(lane, 128)] += jnp.sum(term, axis=0)
        return carry

    lax.fori_loop(0, 20, step, 0)


def conv_back(
    quarter, core, start, wait, before_grad, stats_back, stats, deep, gated, gates, x2, gx3, first, project, mixed, vec,
    gx2, mixed_grad, kept, sent, packed,
    padded, padded_grad, total, acc, both, u_low,
):
    wait(0, 1, 2, 26, 27)
    centred, inverse_root = batch_norm(stats, deep[...], vec)
    shift_sum, gain_sum = collect(stats_back)
    inner = before_grad[...] - shift_sum / FRAMES - centred * (gain_sum / FRAMES)
    low = (inverse_root * row(vec, GAIN + 5) * inner).astype(BF)
    fill(padded_grad, low.astype(F32))
    wait(3)
    start(1)
    fill(padded, gated[...].astype(F32))
    depthwise(padded_grad, vec, total, True)
    tap_grads(padded, padded_grad, acc)
    for tap in range(KERNEL):
        packed[TAP + tap : TAP + tap + 1, :] = column_sum(acc[tap])
    wait(4, 5, 6, 7, 8, 9)
    opened = sigmoid(gates[1].astype(F32))
    passed = total[...] * opened
    both[:, 0:WIDTH] = passed.astype(BF)
    both[:, WIDTH:] = (passed * gates[0].astype(F32) * (1.0 - opened)).astype(BF)
    normed, inverse_root = normalise(x2[...])
    conv_in = (normed * row(vec, GAIN + 2) + row(vec, SHIFT + 2)).astype(BF)
    pieces(core, kept, sent, 192, dot_left(conv_in, lanes(both, quarter * 256, 256)))
    upstream = dot_right(both[:, 0:WIDTH], flat(first[:, 0:16, :]))
    upstream = upstream + dot_right(both[:, WIDTH:], flat(first[:, 16:32, :]))
    packed[GAIN + 2 : GAIN + 3, :] = column_sum(upstream * normed)
    packed[SHIFT + 2 : SHIFT + 3, :] = column_sum(upstream)
    after = gx3[...] + norm_back(upstream, normed, inverse_root, row(vec, GAIN + 2))
    gx2[...] = after
    u_low[...] = after.astype(BF)
    pieces(core, kept, sent, 224, dot_left(mixed[...], lanes(u_low, quarter * 128, 128)))
    mixed_grad[...] = dot_right(u_low[...], flat(project[...])).astype(BF)


def attend_back(
    quarter, core, query_u, query_v, key, value, mixed_grad, probs, offsets, bucket, mixed, inverse,
    three, packed, kept, sent,
    score_grad, all_placed, turned, u_side, v_side, g_side, key_side, value_side, offset_grad,
):
    mirror = mirror_tile()
    above = triangle() >= 0
    left_tile = head_mask(0, TILE)

    def step(pair, carry):
        mine = quarter == pair

        def lane_at(base):
            return pl.ds(pl.multiple_of(base + pair * 128, 128), 128)

        lane = lane_at(0)
        for t in range(4):
            rows = slice(t * TILE, (t + 1) * TILE)
            upstream = (mixed_grad[rows, lane].astype(F32) * inverse[rows, lane]).astype(BF)
            turned[rows, :] = dot(mirror, upstream).astype(BF)
            u_side[:, rows] = dot_left(query_u[rows, lane], mirror).astype(BF)
            v_side[:, rows] = dot_left(query_v[rows, lane], mirror).astype(BF)
            g_side[:, rows] = dot_left(upstream, mirror).astype(BF)

        from_u, from_v = [], []
        for t in range(4):
            rows = slice(t * TILE, (t + 1) * TILE)
            start = LEN - TILE - TILE * t
            window = slice(start, start + SPAN)
            heads = both_heads(turned[rows, :])
            prob_grads = dot_right(heads, value[:, lane])
            mixed_rows = dot(mirror, mixed[rows, lane])
            lows, placed = [], []
            for head in range(2):
                part = slice(head * TILE, head * TILE + TILE)
                weighed = jnp.sum(heads[part].astype(F32) * mixed_rows, axis=1, keepdims=True)
                grad = probs[2 * pair + head, rows, :].astype(F32) * (prob_grads[part] - weighed)
                low = grad.astype(BF)
                score_grad[head, rows, :] = low
                lows.append(low)
                placed.append(unskew(grad, above).astype(BF))
                all_placed[head, rows, :] = placed[head]
            u_parts = dot(jnp.concatenate(lows, axis=0), key[:, lane])
            v_parts = dot(jnp.concatenate(placed, axis=0), offsets[window, lane])

            u_part = jnp.where(left_tile, u_parts[:TILE], u_parts[TILE:]) * 0.125
            v_part = jnp.where(left_tile, v_parts[:TILE], v_parts[TILE:]) * 0.125
            from_u.append(column_sum(u_part))
            from_v.append(column_sum(v_part))
            three[rows, lane] = dot(mirror, (u_part + v_part).astype(BF)).astype(BF)
        for head in range(2):
            side = slice(64 * head, 64 * head + 64)
            key_side[side, :] = dot(u_side[side, :], score_grad[head])
            value_side[side, :] = dot(g_side[side, :], probs[2 * pair + head])
        three[:, lane_at(WIDTH)] = key_side[...].T.astype(BF)
        three[:, lane_at(2 * WIDTH)] = value_side[...].T.astype(BF)
        packed[SHIFT + 6 : SHIFT + 7, lane] = from_u[0] + from_u[1] + from_u[2] + from_u[3]
        packed[SHIFT + 7 : SHIFT + 8, lane] = from_v[0] + from_v[1] + from_v[2] + from_v[3]

        @pl.when(mine)
        def _():
            offset_grad[...] = jnp.zeros_like(offset_grad)
            for t in range(4):
                rows = slice(t * TILE, (t + 1) * TILE)
                window = slice(LEN - TILE - TILE * t, 2 * LEN - TILE * t)
                for head in range(2):
                    side = slice(64 * head, 64 * head + 64)
                    offset_grad[side, window] += dot(v_side[side, rows], all_placed[head, rows, :])
            number = lax.broadcasted_iota(jnp.int32, (2 * LEN, 256), 1)
            chosen = (bucket[...] == number).astype(F32).astype(BF)
            table_grad = dot(offset_grad[...].astype(BF), chosen).T.reshape(32, 8, 128)
            table_grad = jnp.concatenate([table_grad, jnp.zeros((32, 8, 128), F32)], axis=1)
            divide(core, kept, sent, (slice(None), slice(240, 256)), table_grad)

        return carry

    lax.fori_loop(0, 4, step, 0)


def feed_last(
    quarter, core, wait, x1, gx2, project, matrix_in, matrix_out, hidden, x, vec, sums4,
    gx0, kept, sent,
    three, fed, u_low, broad, wide, packed,
):
    own = pl.ds(pl.multiple_of(quarter * TILE, TILE), TILE)
    wait(16, 17, 18, 19, 20, 21, 22, 23, 24)
    normed, inverse_root = normalise(x1[...])
    attn_in = (normed * row(vec, GAIN + 1) + row(vec, SHIFT + 1)).astype(BF)
    pieces(core, kept, sent, 128, dot_left(attn_in, lanes(three, quarter * 384, 384)))
    upstream = dot_right(three[:, 0:WIDTH], flat(project[:, 0:16, :]))
    upstream = upstream + dot_right(three[:, WIDTH : 2 * WIDTH], flat(project[:, 16:32, :]))
    upstream = upstream + dot_right(three[:, 2 * WIDTH :], flat(project[:, 32:48, :]))
    packed[GAIN + 1 : GAIN + 2, :] = column_sum(upstream * normed)
    packed[SHIFT + 1 : SHIFT + 2, :] = column_sum(upstream)
    gx1 = gx2[...] + norm_back(upstream, normed, inverse_root, row(vec, GAIN + 1))
    wide[...] = gx1
    normed, inverse_root = normalise(x[...].astype(F32))
    fed[...] = (normed * row(vec, GAIN) + row(vec, SHIFT)).astype(BF)
    upstream = feed_back(0.5 * gx1, fed, hidden, matrix_in, matrix_out, kept, sent, u_low, broad, quarter, core)
    normed, inverse_root = normalise(x[...].astype(F32))
    packed[GAIN : GAIN + 1, :] = column_sum(upstream * normed)
    packed[SHIFT : SHIFT + 1, :] = column_sum(upstream)
    wide[...] = wide[...] + norm_back(upstream, normed, inverse_root, row(vec, GAIN))
    gx0[...] = wide[own, :]
    for index in range(3):
        packed[GAIN + 3 + index : GAIN + 4 + index, :] = row(sums4, 2 * index)
        packed[SHIFT + 3 + index : SHIFT + 4 + index, :] = row(sums4, 2 * index + 1)
    pieces(core, kept, sent, 176, packed[...].T)


def back(
    where, sums4, bucket_in, stats_back_in, stats_in,
    before_in, deep_in, vec_in, gated_in, gates_in, x2_in, weights, gx3_in, mixed_in,
    u_in, v_in, key_in, value_in, probs_in, offsets_in, x1_in, hidden_in, frames, inverse_in,
    gx0, kept, sent,
    before_grad, deep, vec, gated, gates, x2, first, gx3, last, mixed,
    query_u, query_v, key, value, probs, offsets, x1, project, matrix_in, matrix_out, hidden, x,
    inverse, stats_back, stats, bucket, gx2, mixed_grad, packed, padded, padded_grad, total, acc, both, u_low,
    three, score_grad, all_placed, turned, u_side, v_side, g_side, key_side, value_side, offset_grad,
    fed, broad, wide, arrived,
):
    quarter, core = where[0], where[1]

    def part(at, size):
        return weights.at[:, at : at + size, :]

    start, wait = begin(
        [before_in, deep_in, vec_in, gated_in, gates_in, x2_in, part(320, 32), gx3_in, part(304, 16), mixed_in]
        + [value_in, probs_in, key_in, offsets_in, u_in, v_in]
        + [x1_in, part(256, 48), part(128, 64), hidden_in, frames]
        + [part(16 * j, 16) for j in range(4)]
        + [inverse_in, stats_back_in, stats_in, bucket_in],
        [before_grad, deep, vec, gated, gates, x2, first, gx3, last, mixed]
        + [value, probs, key, offsets, query_u, query_v]
        + [x1, project, matrix_out, hidden, x]
        + [matrix_in.at[:, :, chunk(j)] for j in range(4)]
        + [inverse, stats_back, stats, bucket],
        arrived,
        (26, 27, 2, 0, 1, 3, 4, 5, 6, 7, 8, 9),
        (10, 11, 12, 13, 14, 15, 25, 28),
        (16, 17, 18, 19, 20, 21, 22, 23, 24),
    )
    packed[...] = jnp.zeros_like(packed)
    conv_back(
        quarter, core, start, wait, before_grad, stats_back, stats, deep, gated, gates, x2, gx3, first, last, mixed, vec,
        gx2, mixed_grad, kept, sent, packed,
        padded, padded_grad, total, acc, both, u_low,
    )
    start(2)
    wait(10, 11, 12, 13, 14, 15, 25, 28)
    attend_back(
        quarter, core, query_u, query_v, key, value, mixed_grad, probs, offsets, bucket, mixed, inverse,
        three, packed, kept, sent,
        score_grad, all_placed, turned, u_side, v_side, g_side, key_side, value_side, offset_grad,
    )
    feed_last(
        quarter, core, wait, x1, gx2, project, matrix_in, matrix_out, hidden, x, vec, sums4,
        gx0, kept, sent,
        three, fed, u_low, broad, wide, packed,
    )


def unpack(
    where, part0, part1, part2, part3,
    g_in, g_out, g_project, g_last, g_table, g_first, g_taps, g_conv, g_gain, g_shift,
):
    for hop, part in enumerate((part0, part1, part2, part3)):
        side = lax.rem(where[0] + 4 - hop, 4)

        def put(out, first, rows, wide, lane, m=None, part=part, side=side):
            at = pl.ds(pl.multiple_of(side * wide + lane * 128, 128), 128)
            block = part[first : first + rows, :].astype(F32)
            if m is None:
                out[:, at] = block[0 : out.shape[0]]
            else:
                out[m, :, at] = block

        for m, base in ((0, 0), (1, 256)):
            for lane in range(4):
                put(g_in, base + 16 * lane, 16, 512, lane, m)
            put(g_out, base + 64, 64, 128, 0, m)
        for lane in range(3):
            put(g_project, 128 + 16 * lane, 16, 384, lane)
        for lane in range(2):
            put(g_first, 192 + 16 * lane, 16, 256, lane)
        put(g_last, 224, 16, 128, 0)
        put(g_conv, 384, 16, 128, 0)
        put(g_table, 240, 16, 128, 0)
    vectors = part0[176:192, :].astype(F32)
    g_taps[...] = vectors[:, TAP : TAP + KERNEL]
    vectors = vectors.T
    for index in range(6):
        g_gain[index] = row(vectors, GAIN + index)
    g_shift[...] = vectors[SHIFT : SHIFT + 8]


def whole(shape):
    return pl.BlockSpec(shape, lambda *at: (0,) * len(shape), pipeline_mode=pl.Buffered(1))


WHERE = pl.BlockSpec(memory_space=pltpu.SMEM)
FULL = (LEN, WIDTH)
LIMIT = 56 << 20


ANYWHERE = pl.BlockSpec(memory_space=pl.ANY)


def call(kernel, micros, in_specs, outs, scratch, far=0, semaphores=()):
    return pl.pallas_call(
        kernel,
        grid=(1,),
        in_specs=in_specs,
        out_specs=[ANYWHERE if at < far else whole(shape) for at, (shape, _) in enumerate(outs)],
        out_shape=[jax.ShapeDtypeStruct(shape, dtype) for shape, dtype in outs],
        scratch_shapes=[pltpu.VMEM(shape, dtype) for shape, dtype in scratch]
        + [pltpu.SemaphoreType.DMA((count,)) for count in semaphores],
        compiler_params=pltpu.CompilerParams(vmem_limit_bytes=LIMIT),
        cost_estimate=pl.CostEstimate(flops=micros * 1150 * 10**6, bytes_accessed=0, transcendentals=0),
    )


def share(stats):
    return lax.all_to_all(stats, ("y", "z", "c"), 0, 0, tiled=True)


def with_core(kept, sent):
    other = lax.ppermute(sent, "c", [(0, 1), (1, 0)])
    return (kept.astype(F32) + other.astype(F32)).astype(BF)


def across(chip):
    return lax.all_to_all(chip, ("y", "z"), 0, 0, tiled=True)


def total_of(chip):
    return jnp.sum(chip.astype(F32), axis=0).astype(BF)


def shards(
    inputs, matrices_in, matrices_out, project_in, project_out, pos_table, conv_first, depth_taps,
    conv_last, gain_rows, shift_rows, bucket, cotangent,
):
    fsdp = ("y", "z", "c")
    where = jnp.stack([lax.axis_index("x"), lax.axis_index("c")]).astype(jnp.int32)

    packed = call(
        pack,
        2,
        [whole(part.shape) for part in (matrices_in, matrices_out, project_in, project_out, pos_table, conv_first)]
        + [whole((16, KERNEL)), whole(conv_last.shape), whole(gain_rows.shape), whole(shift_rows.shape)],
        [((400, WIDTH), BF)],
        [((128, 16), F32)],
    )(
        matrices_in, matrices_out, project_in, project_out, pos_table, conv_first,
        jnp.transpose(depth_taps, (0, 2, 1))[0], conv_last, gain_rows, shift_rows,
    )[0]
    weights = lax.all_gather(packed, fsdp, axis=0, tiled=False)
    frames = lax.all_gather(inputs[0], "x", axis=0, tiled=True)
    upstream = lax.all_gather(cotangent[0], "x", axis=0, tiled=True)
    frames, upstream = lax.optimization_barrier((frames, upstream))
    reversed_bucket = jnp.concatenate([bucket[::-1], jnp.full((1,), -1, jnp.int32)])
    tall = reversed_bucket.reshape(2 * LEN, 1)

    full, low, stats_shape = (FULL, F32), (FULL, BF), ((32, 8, 128), F32)
    vec_shape, four = ((128, WIDTH), F32), ((4,) + FULL, BF)
    two, probs_shape, offsets_shape = ((2,) + FULL, BF), ((8, LEN, LEN), BF), ((2 * LEN, WIDTH), BF)
    tall_shape = ((2 * LEN, 1), jnp.int32)

    def rows_of(size):
        return ((32, size, WIDTH), BF)

    held = [full, four, low, low, low, low, vec_shape, probs_shape, low, offsets_shape, full, two, low, full, full]
    broad = ((LEN, 2048), BF)
    wide_in = ((32, 16, 2048), BF)
    (
        x1, hidden, query_u, query_v, key, value, vec, probs, mixed, offsets, x2, gates, gated, deep, inverse, stats,
    ) = call(
        front,
        28,
        [ANYWHERE] * 3,
        held + [stats_shape],
        [low, ((32, 16, 128), BF), wide_in, rows_of(64), rows_of(48), rows_of(16), rows_of(16), rows_of(32), tall_shape]
        + held
        + [low, broad, ((2 * LEN, 256), BF), ((PADDED, WIDTH), F32)],
        far=15,
        semaphores=(12, 15),
    )(frames, weights, tall)
    stats = share(stats)

    gx3, before_grad, y, stats_back, kept4, sent4, sums4 = call(
        centre,
        12,
        [WHERE] + [ANYWHERE] * 6,
        [full, full, ((TILE, WIDTH), BF), stats_shape, ((16, 144, 128), BF), ((16, 144, 128), BF), ((8, WIDTH), F32)],
        [full, vec_shape, full, rows_of(16), wide_in, rows_of(64), low, full, full]
        + [stats_shape, low, four, low, broad, full],
        far=2,
        semaphores=(11, 2),
    )(where, stats, deep, vec, x2, weights, upstream)
    stats_back = share(stats_back)

    gx0, kept, sent = call(
        back,
        42,
        [WHERE, whole((8, WIDTH))] + [ANYWHERE] * 22,
        [((TILE, WIDTH), F32), ((16, 256, 128), BF), ((16, 256, 128), BF)],
        [full, full, vec_shape, low, two, full, rows_of(32), full, rows_of(16), low]
        + [low, low, low, low, probs_shape, offsets_shape, full, rows_of(48), wide_in, rows_of(64), four, low]
        + [full, stats_shape, stats_shape, tall_shape]
        + [full, low, vec_shape, ((PADDED, WIDTH), F32), ((PADDED, WIDTH), F32), full, ((KERNEL, 8, WIDTH), F32)]
        + [((LEN, 2 * WIDTH), BF), low, ((LEN, 3 * WIDTH), BF), two, ((2, LEN, SPAN), BF), ((LEN, 128), BF)]
        + [((128, LEN), BF)] * 3 + [((128, LEN), F32)] * 2 + [((128, 2 * LEN), F32)]
        + [low, broad, full],
        semaphores=(29,),
    )(
        where, sums4, tall, stats_back, stats,
        before_grad, deep, vec, gated, gates, x2, weights, gx3, mixed,
        query_u, query_v, key, value, probs, offsets, x1, hidden, frames, inverse,
    )
    chips = [with_core(kept, sent), with_core(kept4, sent4)]
    total = total_of(across(jnp.concatenate(chips, axis=1)))
    hops = [[(i, (i + hop) % 4) for i in range(4)] for hop in range(4)]
    parts = [total] + [lax.ppermute(total, "x", hops[hop]) for hop in (1, 2, 3)]
    results = call(
        unpack,
        2,
        [WHERE] + [whole(total.shape)] * 4,
        [((2, 16, 2048), F32), ((2, 64, 512), F32), ((16, 1536), F32), ((16, 512), F32), ((8, 512), F32),
         ((16, 1024), F32), ((16, KERNEL), F32), ((16, 512), F32), ((6, 1, 16), F32), ((8, 16), F32)],
        [],
    )(where, *parts)
    results = list(results)
    results[6] = results[6].T
    results[8] = results[8][:, 0]
    return (y[None], gx0[None]) + tuple(result[None] for result in results)


def solution(mesh):
    fine = Mesh(mesh.devices.reshape(4, 4, 2, 4), ("y", "z", "c", "x"))
    fsdp = ("y", "z", "c")
    activations = P(fsdp, "x", None)
    placed = (
        activations,
        P(None, None, fsdp, None),
        P(None, None, fsdp, None),
        P(None, fsdp, None),
        P(None, fsdp, None),
        P(None, fsdp, None),
        P(None, fsdp, None),
        P(None, None, fsdp),
        P(None, fsdp, None),
        P(None, None, fsdp),
        P(None, None, fsdp),
    )
    return jax.shard_map(
        shards,
        mesh=fine,
        in_specs=placed + (P(), activations),
        out_specs=(activations, activations) + placed[1:],
        check_vma=False,
    )
```
